32 devices in a mesh: fsdp: 8 (over z, core), ctx: 2 (over x), tp: 2 (over y).
Axes of the slice: x: 2, y: 2, z: 4, core: 2. Of those that a mesh axis runs over, the one named last changes fastest.
Arguments:
- image_tokens: bfloat16 [16, 1152, 1536], P('fsdp', 'ctx'), may hold values from -6 to 6
- text_tokens: bfloat16 [16, 176, 1536], P('fsdp', 'ctx'), may hold values from -6 to 6
- cond_vector: bfloat16 [16, 1536], P(None, 'fsdp'), may hold values from -6 to 6
- image_cotangent: bfloat16 [16, 1152, 1536], P('fsdp', 'ctx'), may hold values from -6 to 6
- text_cotangent: bfloat16 [16, 176, 1536], P('fsdp', 'ctx'), may hold values from -6 to 6
- image_counts: int32 [16, 2], P('fsdp'), may hold values from 1 to 576, 1024 in all within a row
- text_counts: int32 [16, 2], P('fsdp'), may hold values from 1 to 88, 154 in all within a row
- seq_live: int32 [16], replicated, may hold values 0 or 1
- ada_weight: bfloat16 [2, 1536, 9216], P(None, 'fsdp', 'tp'), may hold values from -0.15625 to 0.15625
- ada_bias: bfloat16 [2, 9216], P(None, 'tp'), may hold values from -3 to 3
- qkv_weight: bfloat16 [2, 1536, 3, 1536], P(None, 'fsdp', None, 'tp'), may hold values from -0.15625 to 0.15625
- qv_bias: bfloat16 [2, 2, 1536], P(None, None, 'tp'), may hold values from -3 to 3
- attn_out_weight: bfloat16 [2, 1536, 1536], P(None, 'tp', 'fsdp'), may hold values from -2.5 to 2.5
- attn_out_bias: bfloat16 [2, 1536], replicated, may hold values from -3 to 3
- mlp_up_weight: bfloat16 [2, 1536, 6144], P(None, 'fsdp', 'tp'), may hold values from -0.15625 to 0.15625
- mlp_up_bias: bfloat16 [2, 6144], P(None, 'tp'), may hold values from -3 to 3
- mlp_down_weight: bfloat16 [2, 6144, 1536], P(None, 'tp', 'fsdp'), may hold values from -0.078125 to 0.078125
- mlp_down_bias: bfloat16 [2, 1536], replicated, may hold values from -3 to 3
Outputs:
- image_output: bfloat16 [16, 1152, 1536], P('fsdp', 'ctx')
- text_output: bfloat16 [16, 176, 1536], P('fsdp', 'ctx')
- image_grad: bfloat16 [16, 1152, 1536], P('fsdp', 'ctx')
- text_grad: bfloat16 [16, 176, 1536], P('fsdp', 'ctx')
- cond_grad: float32 [16, 1536], P(None, 'fsdp')
- ada_weight_grad: float32 [2, 1536, 9216], P(None, 'fsdp', 'tp')
- ada_bias_grad: float32 [2, 9216], P(None, 'tp')
- qkv_weight_grad: float32 [2, 1536, 3, 1536], P(None, 'fsdp', None, 'tp')
- qv_bias_grad: float32 [2, 2, 1536], P(None, None, 'tp')
- attn_out_weight_grad: float32 [2, 1536, 1536], P(None, 'tp', 'fsdp')
- attn_out_bias_grad: float32 [2, 1536], replicated
- mlp_up_weight_grad: float32 [2, 1536, 6144], P(None, 'fsdp', 'tp')
- mlp_up_bias_grad: float32 [2, 6144], P(None, 'tp')
- mlp_down_weight_grad: float32 [2, 6144, 1536], P(None, 'tp', 'fsdp')
- mlp_down_bias_grad: float32 [2, 1536], replicated
The draws below stay inside these ranges and needn't reach their ends.
Inputs may be any that keep to these rules, and one draw needn't show every extreme that they name: `image_counts`: each row sums to 1024. `text_counts`: each row sums to 154.
All inputs are finite; a program needn't handle non-finite values.
Results may differ from the reference program's by a relative error of at most 0.01895.
Values may be sent and summed in bfloat16 or wider, within the bound.
No kernel may reach another device: no remote copies, remote signals or barrier semaphores. Data moves between devices by JAX's collectives and lax.ppermute only.
A program may use at most 640 MiB of HBM per device.

```python
import math
import jax
import jax.numpy as jnp
import numpy as np
from jax import lax

D = 1536
HEADS = 24
HEAD = 64
FF = 6144
IMG = 1024
TXT = 154
MB = 2
SLOTS = 1
SEQS = 16
ICAP = 576
TCAP = 88
N_CTX = 2


def set_ends(drawn, key, low, high):
    spot = [jax.random.randint(jax.random.fold_in(key, axis), (), 0, length) for axis, length in enumerate(drawn.shape)]
    widest = drawn.shape.index(max(drawn.shape))
    neighbour = spot[:widest] + [(spot[widest] + 1) % drawn.shape[widest]] + spot[widest + 1:]
    return drawn.at[tuple(spot)].set(low).at[tuple(neighbour)].set(high)


def block_scale(own_key, extent, shards, smallest, largest):
    gain, own = 1.0, jax.random.fold_in(own_key, 6)
    for axis_at, shards_of in shards:
        draws = jnp.exp(jax.random.uniform(jax.random.fold_in(own, axis_at), (shards_of,), jnp.float32, smallest / len(shards), largest / len(shards)))
        gain = gain * jnp.repeat(draws, extent[axis_at] // shards_of).reshape([-1 if axis == axis_at else 1 for axis in range(len(extent))])
    return gain


def profile(number_of, total, bound, lean):
    loads = [(1 << 20) // math.isqrt(standing ** lean) + 1 for standing in range(2, number_of + 1)]
    surplus, holding = total - bound - (number_of - 1), [1] * (number_of - 1)
    while surplus > 0:
        candidates = [i for i in range(number_of - 1) if holding[i] < bound]
        whole, left = sum([loads[i] for i in candidates]), surplus
        for i in candidates:
            extra = min(bound - holding[i], max(1, left * loads[i] // whole), surplus)
            holding[i] = holding[i] + extra
            surplus = surplus - extra
    return np.array([bound] + holding)


def ragged_sizes(own_key, number_of, total, most, slope):
    if number_of == 2:
        one = jax.random.randint(own_key, (), max(1, total - most), min(most, total - 1) + 1)
        return jnp.stack([one, total - one])
    sizes = jnp.asarray(profile(number_of, total, most, slope), jnp.int32)
    couples = (number_of - 1) // 2
    source_of, receiver = sizes[1:1 + 2 * couples:2], sizes[2:2 + 2 * couples:2]
    margin = jnp.minimum(source_of - 1, most - receiver)
    shifted = jax.random.randint(jax.random.fold_in(own_key, 1), (couples,), 0, 1 << 20) % (margin + 1)
    sizes = sizes.at[1:1 + 2 * couples:2].set(source_of - shifted).at[2:2 + 2 * couples:2].set(receiver + shifted)
    return sizes[jax.random.permutation(jax.random.fold_in(own_key, 2), number_of)]


def normal_values(rng, shape, spread, reach, cuts=(), held_as=jnp.bfloat16):
    result = spread * jax.random.normal(rng, shape, jnp.float32)
    if cuts:
        result = result * block_scale(rng, shape, cuts, -0.22, 0.18)
    return jnp.clip(result, -reach, reach).astype(held_as)


def setup_inputs(seed: int = 0) -> dict:
    key_list = jax.random.split(jax.random.key(seed), 19)
    return {
        "image_tokens": normal_values(key_list[0], (SEQS, N_CTX * ICAP, D), 1.0, 6.0, ((0, 8), (1, 2))),
        "text_tokens": normal_values(key_list[1], (SEQS, N_CTX * TCAP, D), 1.0, 6.0, ((0, 8), (1, 2))),
        "cond_vector": normal_values(key_list[2], (SEQS, D), 1.0, 6.0, ((1, 8),)),
        "image_cotangent": normal_values(key_list[3], (SEQS, N_CTX * ICAP, D), 1.0, 6.0, ((0, 8), (1, 2))),
        "text_cotangent": normal_values(key_list[4], (SEQS, N_CTX * TCAP, D), 1.0, 6.0, ((0, 8), (1, 2))),
        "image_counts": jax.vmap(lambda own: ragged_sizes(own, N_CTX, IMG, ICAP, 1))(jax.random.split(key_list[5], SEQS)).reshape((SEQS, N_CTX)).astype(jnp.int32),
        "text_counts": jax.vmap(lambda own: ragged_sizes(own, N_CTX, TXT, TCAP, 1))(jax.random.split(key_list[6], SEQS)).reshape((SEQS, N_CTX)).astype(jnp.int32),
        "seq_live": set_ends((jax.random.randint(key_list[7], (SEQS,), 0, 4) < 3).astype(jnp.int32), jax.random.fold_in(key_list[7], 1), 0, 1),
        "ada_weight": normal_values(key_list[8], (2, D, 6 * D), D ** -0.5, 0.15625, ((1, 8), (2, 2))),
        "ada_bias": normal_values(key_list[9], (2, 6 * D), 0.5, 3.0, ((1, 2),)),
        "qkv_weight": normal_values(key_list[10], (2, D, 3, D), D ** -0.5, 0.15625, ((1, 8), (3, 2))),
        "qv_bias": normal_values(key_list[11], (2, 2, D), 0.5, 3.0, ((2, 2),)),
        "attn_out_weight": normal_values(key_list[12], (2, D, D), (max(D // 256, 1)) ** -0.5, 2.5, ((1, 2), (2, 8))),
        "attn_out_bias": normal_values(key_list[13], (2, D), 0.5, 3.0),
        "mlp_up_weight": normal_values(key_list[14], (2, D, FF), D ** -0.5, 0.15625, ((1, 8), (2, 2))),
        "mlp_up_bias": normal_values(key_list[15], (2, FF), 0.5, 3.0, ((1, 2),)),
        "mlp_down_weight": normal_values(key_list[16], (2, FF, D), FF ** -0.5, 0.078125, ((1, 2), (2, 8))),
        "mlp_down_bias": normal_values(key_list[17], (2, D), 0.5, 3.0),
    }


@jax.custom_vjp
def low(v):
    return lax.optimization_barrier(v.astype(jnp.bfloat16)).astype(jnp.float32)

@jax.custom_vjp
def low_back(v):
    return v

def low_keep(v):
    return (low(v), None)

def low_pass(kept, grad):
    return (grad,)

def back_keep(v):
    return (v, None)

def back_low(kept, grad):
    return (low(grad),)
low.defvjp(low_keep, low_pass)
low_back.defvjp(back_keep, back_low)
HIGHEST = lax.Precision.HIGHEST

def layer_norm(values):
    row_mean = lax.optimization_barrier(jnp.mean(values, axis=-1, keepdims=True))
    centred = values - row_mean
    return centred * lax.rsqrt(lax.optimization_barrier(jnp.mean(centred * centred, axis=-1, keepdims=True)) + 1e-06)

def attend_head(queries, key_rows, value_rows, live_mask):
    scores = low_back(jnp.dot(queries, key_rows.T, precision=HIGHEST) * HEAD ** (-0.5))
    scores = jnp.where(live_mask[None, :] > 0, scores, -1e+30)
    row_top = lax.optimization_barrier(jnp.max(scores, axis=-1, keepdims=True))
    exponent = jnp.exp(scores - row_top)
    probs = exponent / lax.optimization_barrier(jnp.sum(exponent, axis=-1, keepdims=True))
    return jnp.dot(low(probs), value_rows, precision=HIGHEST)

def block_forward(params, image_rows, text_rows, cond_row, live_mask):
    ada_weight, ada_bias, qkv_weight, qv_bias, attn_out_weight, attn_out_bias, mlp_up_weight, mlp_up_bias, mlp_down_weight, mlp_down_bias = params
    activated = low(jax.nn.silu(cond_row))
    modulation = low_back(jnp.einsum('d,tde->te', activated, ada_weight, precision=HIGHEST)) + ada_bias
    modulation = modulation.reshape(2, 6, D)
    inputs = (image_rows, text_rows)
    query_parts, key_parts, value_parts = ([], [], [])
    for stream in range(2):
        normed = low(layer_norm(inputs[stream]) * (1.0 + modulation[stream, 1]) + modulation[stream, 0])
        projected = low_back(jnp.einsum('rd,dke->rke', normed, qkv_weight[stream], precision=HIGHEST))
        query_parts.append(low(projected[:, 0] + qv_bias[stream, 0]))
        key_parts.append(low(projected[:, 1]))
        value_parts.append(low(projected[:, 2] + qv_bias[stream, 1]))
    queries = jnp.concatenate(query_parts, axis=0)
    key_rows = jnp.concatenate(key_parts, axis=0)
    value_rows = jnp.concatenate(value_parts, axis=0)
    total_rows = queries.shape[0]

    def split_heads(matrix):
        return matrix.reshape(total_rows, HEADS, HEAD).transpose(1, 0, 2)
    attended = lax.map(lambda items: jax.checkpoint(attend_head)(items[0], items[1], items[2], live_mask), (split_heads(queries), split_heads(key_rows), split_heads(value_rows)))
    attended = low_back(low(attended.transpose(1, 0, 2).reshape(total_rows, D)))
    image_count = image_rows.shape[0]
    pieces = (attended[:image_count], attended[image_count:])
    results = []
    for stream in range(2):
        att_value = low_back(jnp.dot(pieces[stream], attn_out_weight[stream], precision=HIGHEST)) + attn_out_bias[stream]
        middle = inputs[stream] + modulation[stream, 2] * att_value
        normed = low(layer_norm(middle) * (1.0 + modulation[stream, 4]) + modulation[stream, 3])
        pre_act = low_back(jnp.dot(normed, mlp_up_weight[stream], precision=HIGHEST)) + mlp_up_bias[stream]
        activ = low(jax.nn.gelu(pre_act, approximate=True))
        mlp_value = low_back(jnp.dot(activ, mlp_down_weight[stream], precision=HIGHEST)) + mlp_down_bias[stream]
        results.append(middle + modulation[stream, 5] * mlp_value)
    return (results[0], results[1])

def reference(image_tokens, text_tokens, cond_vector, image_cotangent, text_cotangent, image_counts, text_counts, seq_live, ada_weight, ada_bias, qkv_weight, qv_bias, attn_out_weight, attn_out_bias, mlp_up_weight, mlp_up_bias, mlp_down_weight, mlp_down_bias):
    params = tuple((weight.astype(jnp.float32) for weight in (ada_weight, ada_bias, qkv_weight, qv_bias, attn_out_weight, attn_out_bias, mlp_up_weight, mlp_up_bias, mlp_down_weight, mlp_down_bias)))
    group_slots = MB * SLOTS
    live_all = seq_live.astype(jnp.float32)
    batch_index = jnp.arange(SEQS, dtype=jnp.int32) % group_slots // SLOTS
    marked = (batch_index[:, None] == jnp.arange(MB, dtype=jnp.int32)[None, :]).astype(jnp.float32) * live_all[:, None]
    members = lax.optimization_barrier(jnp.sum(marked, axis=0))
    shares = jnp.sum(live_all) / (MB * jnp.maximum(members, 1.0))
    seq_weights = lax.optimization_barrier(jnp.sum(marked * shares[None, :], axis=1))
    image_slot = jnp.arange(N_CTX * ICAP, dtype=jnp.int32) % ICAP
    text_slot = jnp.arange(N_CTX * TCAP, dtype=jnp.int32) % TCAP
    image_live = (image_slot[None, :] < jnp.repeat(image_counts, ICAP, axis=1)).astype(jnp.float32)
    text_live = (text_slot[None, :] < jnp.repeat(text_counts, TCAP, axis=1)).astype(jnp.float32)

    def step(totals, items):
        image_rows, text_rows, cond_row, image_cot, text_cot, image_mask, text_mask, weight, alive = items
        live_mask = jnp.concatenate([image_mask, text_mask], axis=0)

        def run(weights, image_in, text_in, cond_in):
            return block_forward(weights, image_in, text_in, cond_in, live_mask)
        outputs, pull = jax.vjp(run, params, image_rows, text_rows, cond_row)
        grads = pull((image_cot * image_mask[:, None] * weight, text_cot * text_mask[:, None] * weight))
        totals = jax.tree.map(lambda total, grad: total + grad, totals, grads[0])
        return (totals, (outputs[0] * image_mask[:, None] * alive, outputs[1] * text_mask[:, None] * alive, grads[1], grads[2], grads[3]))
    zeros = jax.tree.map(jnp.zeros_like, params)
    totals, stacked = lax.scan(step, zeros, (image_tokens.astype(jnp.float32), text_tokens.astype(jnp.float32), cond_vector.astype(jnp.float32), image_cotangent.astype(jnp.float32), text_cotangent.astype(jnp.float32), image_live, text_live, seq_weights, live_all))
    return (stacked[0].astype(jnp.bfloat16), stacked[1].astype(jnp.bfloat16), stacked[2].astype(jnp.bfloat16), stacked[3].astype(jnp.bfloat16), stacked[4], totals[0], totals[1], totals[2], totals[3], totals[4], totals[5], totals[6], totals[7], totals[8], totals[9])
```

```python
import functools

import jax
import jax.numpy as jnp
from jax import lax
from jax.experimental import pallas as pl
from jax.experimental.pallas import tpu as pltpu
from jax.sharding import Mesh
from jax.sharding import PartitionSpec as P

D = 1536
HEAD = 64
LANES = 128
MB = 2
F32 = jnp.float32
BF16 = jnp.bfloat16
FSDP = ("z", "core")
PAIR = ((0, 1), (1, 0))
DEAD = -1e30


def swap(values, axis):
    return lax.ppermute(values, axis, PAIR)


def pair_sum(values, axis):
    mine = values.astype(BF16)
    return mine.astype(F32) + swap(mine, axis).astype(F32)


def ctx_sum(values):
    if lax.axis_size("ctx") == 2:
        return pair_sum(values, "ctx")
    return lax.psum(values.astype(BF16), "ctx").astype(F32)


def dot(left, right):
    return lax.dot_general(left, right, (((1,), (0,)), ((), ())), preferred_element_type=F32)


def dot_nt(left, right):
    return lax.dot_general(left, right, (((1,), (1,)), ((), ())), preferred_element_type=F32)


def dot_tn(left, right):
    return lax.dot_general(left, right, (((0,), (0,)), ((), ())), preferred_element_type=F32)


def gather_rows(shard):
    streams, rows, columns = shard.shape
    if lax.axis_size("ctx") == 2:
        piece = lax.dynamic_index_in_dim(shard, lax.axis_index("ctx"), 0, keepdims=False)
        whole = lax.all_gather(piece, ("ctx",) + FSDP, axis=0, tiled=True)
        return whole.reshape(streams, -1, columns)
    return lax.all_gather(shard, FSDP, axis=1, tiled=True)


def reduce_rows(part):
    own = lax.psum_scatter(part.astype(BF16), FSDP, scatter_dimension=0, tiled=True)
    return ctx_sum(own)


def scatter_groups(parts):
    z_count = lax.axis_size("z")
    z_index, core = lax.axis_index("z"), lax.axis_index("core")
    split = parts.reshape((z_count, 2) + parts.shape[1:])
    keep = lax.dynamic_index_in_dim(split, core, 1, keepdims=False)
    give = lax.dynamic_index_in_dim(split, 1 - core, 1, keepdims=False)
    chip = keep + swap(give, "core")
    total = lax.dynamic_index_in_dim(chip, z_index, 0, keepdims=False)
    for step in range(1, z_count):
        target = lax.rem(z_index + step, z_count)
        sent = lax.dynamic_index_in_dim(chip, target, 0, keepdims=False)
        total = total + lax.ppermute(
            sent, "z", [(index, (index + step) % z_count) for index in range(z_count)]
        )
    return total


def normalise(values):
    row_mean = jnp.mean(values, axis=-1, keepdims=True)
    centred = values - row_mean
    inverse = lax.rsqrt(jnp.mean(centred * centred, axis=-1, keepdims=True) + 1e-06)
    return centred * inverse, inverse


def modulate(values, shift, scale):
    return normalise(values)[0] * (1.0 + scale) + shift


def modulate_back(values, scale, grad):
    unit, inverse = normalise(values)
    unit_grad = grad * (1.0 + scale)
    first = jnp.mean(unit_grad, axis=-1, keepdims=True)
    second = jnp.mean(unit_grad * unit, axis=-1, keepdims=True)
    back = inverse * (unit_grad - first - unit * second)
    return back, jnp.sum(grad, axis=1), jnp.sum(grad * unit, axis=1)


def gelu_tanh(values):
    return jax.nn.gelu(values, approximate=True)


def masked_pair(image, text, stacked, scale):
    first = lax.broadcasted_iota(jnp.int32, (1, LANES), 1) < HEAD
    rows = image.shape[0]
    half = rows + text.shape[0]
    for head in range(2):
        kept = first if head == 0 else jnp.logical_not(first)
        base = head * half
        stacked[base : base + rows] = jnp.where(kept, image * scale, 0.0).astype(BF16)
        stacked[base + rows : base + half] = jnp.where(kept, text * scale, 0.0).astype(BF16)


def unstack(pair):
    first = lax.broadcasted_iota(jnp.int32, (1, LANES), 1) < HEAD
    turned = pair.T
    half = turned.shape[0] // 2
    return jnp.where(first, turned[:half], turned[half:])


def attend_kernel(parts, image_rows, *refs):
    query_image, query_text = refs[0], refs[1]
    key_refs = refs[2 : 2 + parts]
    value_refs = refs[2 + parts : 2 + 2 * parts]
    bias_refs = refs[2 + 2 * parts : 2 + 3 * parts]
    out_image, out_text, log_ref, queries, scores = refs[2 + 3 * parts :]
    masked_pair(
        query_image[...].astype(F32), query_text[...].astype(F32), queries, HEAD ** (-0.5)
    )
    stacked = queries[...]
    top = None
    base = 0
    for part in range(parts):
        rows = key_refs[part].shape[0]
        score = dot_nt(key_refs[part][...], stacked) + bias_refs[part][...]
        scores[base : base + rows] = score
        part_top = jnp.max(score, axis=0, keepdims=True)
        top = part_top if top is None else jnp.maximum(top, part_top)
        base += rows
    total = jnp.zeros_like(top)
    attended = jnp.zeros((LANES, stacked.shape[0]), F32)
    base = 0
    for part in range(parts):
        rows = key_refs[part].shape[0]
        exponent = jnp.exp(scores[base : base + rows] - top)
        total = total + jnp.sum(exponent, axis=0, keepdims=True)
        attended = attended + dot_tn(value_refs[part][...], exponent.astype(BF16))
        base += rows
    result = unstack(attended / total)
    out_image[...] = result[:image_rows].astype(BF16)
    out_text[...] = result[image_rows:].astype(BF16)
    log_ref[...] = top + jnp.log(total)


def attend_back_kernel(streams, image_rows, *refs):
    parts = len(streams)
    query_image, query_text, out_image, out_text, grad_image, grad_text, log_ref = refs[:7]
    key_refs = refs[7 : 7 + parts]
    value_refs = refs[7 + parts : 7 + 2 * parts]
    bias_refs = refs[7 + 2 * parts : 7 + 3 * parts]
    rest = refs[7 + 3 * parts :]
    query_grad_image, query_grad_text, query_sum, value_sum = rest[:4]
    pair_grads = rest[4 : 4 + parts]
    queries, grads, products = rest[4 + parts :]
    masked_pair(
        query_image[...].astype(F32), query_text[...].astype(F32), queries, HEAD ** (-0.5)
    )
    grad_rows_image, grad_rows_text = grad_image[...].astype(F32), grad_text[...].astype(F32)
    masked_pair(grad_rows_image, grad_rows_text, grads, 1.0)
    first = lax.broadcasted_iota(jnp.int32, (1, LANES), 1) < HEAD
    product_image = grad_rows_image * out_image[...].astype(F32)
    product_text = grad_rows_text * out_text[...].astype(F32)
    half = product_image.shape[0] + product_text.shape[0]
    for head in range(2):
        kept = first if head == 0 else jnp.logical_not(first)
        base = head * half
        products[base : base + image_rows] = jnp.where(kept, product_image, 0.0)
        products[base + image_rows : base + half] = jnp.where(kept, product_text, 0.0)
    inner = jnp.sum(products[...].T, axis=0, keepdims=True)
    stacked, grad_stacked = queries[...], grads[...]
    log_total = log_ref[...]
    query_grad = jnp.zeros((LANES, stacked.shape[0]), F32)
    value_totals = [jnp.zeros((1, LANES), F32) for _ in range(2)]
    for part in range(parts):
        keys, values = key_refs[part][...], value_refs[part][...]
        probs = jnp.exp(dot_nt(keys, stacked) + bias_refs[part][...] - log_total)
        grad_probs = dot_nt(values, grad_stacked)
        grad_scores = (probs * (grad_probs - inner)).astype(BF16)
        value_grad = dot(probs.astype(BF16), grad_stacked)
        pair_grads[part][1] = value_grad.astype(BF16)
        stream = streams[part]
        value_totals[stream] = value_totals[stream] + jnp.sum(value_grad, axis=0, keepdims=True)
        pair_grads[part][0] = dot(grad_scores, stacked).astype(BF16)
        query_grad = query_grad + dot_tn(keys, grad_scores)
    result = unstack(query_grad) * HEAD ** (-0.5)
    query_grad_image[...] = result[:image_rows].astype(BF16)
    query_grad_text[...] = result[image_rows:].astype(BF16)
    query_sum[0:1] = jnp.sum(result[:image_rows], axis=0, keepdims=True)
    query_sum[1:2] = jnp.sum(result[image_rows:], axis=0, keepdims=True)
    for stream in range(2):
        value_sum[stream : stream + 1] = value_totals[stream]


def block_of(slot, rows, base=0):
    return pl.BlockSpec((None, rows, LANES), lambda pair: (slot, 0, base + pair))


def flat_block(rows, base=0):
    return pl.BlockSpec((rows, LANES), lambda pair: (0, base + pair))


def column_block(rows):
    return pl.BlockSpec((rows, 1), lambda pair: (0, 0))


def key_specs(slot, key_parts, pairs):
    keys, values, biases = [], [], []
    for rows_array, _, here, _ in key_parts:
        rows = rows_array.shape[-2]
        if here:
            keys.append(block_of(slot, rows))
            values.append(block_of(slot, rows, pairs))
        else:
            keys.append(flat_block(rows))
            values.append(flat_block(rows, pairs))
        biases.append(column_block(rows))
    return keys + values + biases


def key_operands(key_parts):
    arrays = [part[0] for part in key_parts]
    return arrays + arrays + [part[1] for part in key_parts]


def attend(slot, queries, key_parts):
    image, text = queries
    image_rows, text_rows = image.shape[1], text.shape[1]
    width = image.shape[2]
    pairs = width // LANES
    stacked = 2 * (image_rows + text_rows)
    key_rows = sum(part[0].shape[-2] for part in key_parts)
    return pl.pallas_call(
        functools.partial(attend_kernel, len(key_parts), image_rows),
        grid=(pairs,),
        in_specs=[block_of(slot, image_rows), block_of(slot, text_rows)]
        + key_specs(slot, key_parts, pairs),
        out_specs=[
            flat_block(image_rows),
            flat_block(text_rows),
            pl.BlockSpec((None, 1, stacked), lambda pair: (pair, 0, 0)),
        ],
        out_shape=[
            jax.ShapeDtypeStruct((image_rows, width), BF16),
            jax.ShapeDtypeStruct((text_rows, width), BF16),
            jax.ShapeDtypeStruct((pairs, 1, stacked), F32),
        ],
        scratch_shapes=[
            pltpu.VMEM((stacked, LANES), BF16),
            pltpu.VMEM((key_rows, stacked), F32),
        ],
        compiler_params=pltpu.CompilerParams(vmem_limit_bytes=48 * 1024 * 1024),
        cost_estimate=pl.CostEstimate(
            flops=pairs * 4 * key_rows * stacked * 4 * LANES,
            bytes_accessed=2 * width * (2 * image_rows + 2 * key_rows),
            transcendentals=pairs * key_rows * stacked,
        ),
        name="attend",
    )(image, text, *key_operands(key_parts))


def attend_back(slot, queries, outs, grads, log_total, key_parts):
    image, text = queries
    image_rows, text_rows = image.shape[1], text.shape[1]
    width = image.shape[2]
    pairs = width // LANES
    stacked = 2 * (image_rows + text_rows)
    key_rows = sum(part[0].shape[-2] for part in key_parts)
    part_rows = [part[0].shape[-2] for part in key_parts]
    row_blocks = [block_of(slot, image_rows), block_of(slot, text_rows)]
    sum_block = pl.BlockSpec((None, 2, LANES), lambda pair: (pair, 0, 0))
    sum_shape = jax.ShapeDtypeStruct((pairs, 2, LANES), F32)
    return pl.pallas_call(
        functools.partial(
            attend_back_kernel, tuple(part[3] for part in key_parts), image_rows
        ),
        grid=(pairs,),
        in_specs=row_blocks
        + [flat_block(image_rows), flat_block(text_rows)]
        + row_blocks
        + [pl.BlockSpec((None, 1, stacked), lambda pair: (pair, 0, 0))]
        + key_specs(slot, key_parts, pairs),
        out_specs=[flat_block(image_rows), flat_block(text_rows), sum_block, sum_block]
        + [pl.BlockSpec((2, rows, LANES), lambda pair: (0, 0, pair)) for rows in part_rows],
        out_shape=[
            jax.ShapeDtypeStruct((image_rows, width), BF16),
            jax.ShapeDtypeStruct((text_rows, width), BF16),
            sum_shape,
            sum_shape,
        ]
        + [jax.ShapeDtypeStruct((2, rows, width), BF16) for rows in part_rows],
        scratch_shapes=[
            pltpu.VMEM((stacked, LANES), BF16),
            pltpu.VMEM((stacked, LANES), BF16),
            pltpu.VMEM((stacked, LANES), F32),
        ],
        compiler_params=pltpu.CompilerParams(vmem_limit_bytes=48 * 1024 * 1024),
        cost_estimate=pl.CostEstimate(
            flops=pairs * 10 * key_rows * stacked * 4 * LANES,
            bytes_accessed=2 * width * (4 * image_rows + 4 * key_rows),
            transcendentals=pairs * key_rows * stacked,
        ),
        name="attend_back",
    )(image, text, outs[0], outs[1], grads[0], grads[1], log_total, *key_operands(key_parts))


def on_device(
    image_tokens,
    text_tokens,
    cond_vector,
    image_cotangent,
    text_cotangent,
    image_counts,
    text_counts,
    seq_live,
    ada_weight,
    ada_bias,
    qkv_weight,
    qv_bias,
    attn_out_weight,
    attn_out_bias,
    mlp_up_weight,
    mlp_up_bias,
    mlp_down_weight,
    mlp_down_bias,
):
    slot_count = image_tokens.shape[0]
    per_batch = slot_count // MB
    seq_count = seq_live.shape[0]
    cap_image = image_tokens.shape[1]
    cap_text = text_tokens.shape[1]
    text_rows = -(-cap_text // 16) * 16
    extra = ((0, 0), (0, text_rows - cap_text), (0, 0))
    caps = (cap_image, text_rows)
    group_index = lax.axis_index("z") * 2 + lax.axis_index("core")
    ctx_count = lax.axis_size("ctx")
    ctx_index = lax.axis_index("ctx")
    tp_index = lax.axis_index("tp")
    spans = 6 // lax.axis_size("tp")
    rows_local = ada_weight.shape[1]
    width = qkv_weight.shape[3]

    kv_full = gather_rows(qkv_weight[:, :, 1:].reshape(2, rows_local, 2 * width))
    q_full = gather_rows(qkv_weight[:, :, 0])
    out_full = gather_rows(jnp.swapaxes(attn_out_weight, 1, 2))
    up_full = gather_rows(mlp_up_weight)
    down_full = gather_rows(jnp.swapaxes(mlp_down_weight, 1, 2))

    live_all = seq_live.astype(F32)
    batch_index = jnp.arange(seq_count, dtype=jnp.int32) % slot_count // per_batch
    marked = (batch_index[:, None] == jnp.arange(MB, dtype=jnp.int32)[None, :]).astype(
        F32
    ) * live_all[:, None]
    members = jnp.sum(marked, axis=0)
    shares = jnp.sum(live_all) / (MB * jnp.maximum(members, 1.0))
    seq_weights = jnp.sum(marked * shares[None, :], axis=1)
    own_weights = lax.dynamic_slice_in_dim(seq_weights, group_index * slot_count, slot_count)
    own_live = lax.dynamic_slice_in_dim(live_all, group_index * slot_count, slot_count)

    cond_float = cond_vector.astype(F32)
    activated = jax.nn.silu(cond_float).astype(BF16)
    ada_local = ada_weight.reshape(2, rows_local, spans, D)
    ada_partial = jnp.einsum("sd,tdke->stke", activated, ada_local, preferred_element_type=F32)
    mod_half = scatter_groups(
        ada_partial.reshape(seq_count // slot_count, slot_count, 2, spans, D)
    ) + ada_bias.reshape(1, 2, spans, D)
    mod_other = swap(mod_half, "tp")
    modulation = jnp.where(
        tp_index == 0,
        jnp.concatenate([mod_half, mod_other], axis=2),
        jnp.concatenate([mod_other, mod_half], axis=2),
    )

    counts = (image_counts, text_counts)
    live_rows = []
    key_bias = []
    for stream in range(2):
        places = jnp.arange(caps[stream], dtype=jnp.int32)
        own_counts = lax.dynamic_slice_in_dim(counts[stream], ctx_index, 1, 1)
        live_rows.append((places[None, :] < own_counts).astype(F32)[:, :, None])
        key_bias.append(
            jnp.where(
                places[None, None, :, None] < counts[stream][:, :, None, None], 0.0, DEAD
            ).astype(F32)
        )
    tokens = (image_tokens, jnp.pad(text_tokens, extra))
    cotangents = (image_cotangent, jnp.pad(text_cotangent, extra))

    def mod_of(stream, which):
        return modulation[:, stream, which][:, None, :]

    def flat(values):
        return values.reshape(-1, values.shape[-1])

    def tall(stream, values):
        return values.reshape(slot_count, caps[stream], values.shape[-1])

    inputs = [part.astype(F32) for part in tokens]
    hidden_in, queries, key_values = [], [], []
    for stream in range(2):
        normed = flat(
            modulate(inputs[stream], mod_of(stream, 0), mod_of(stream, 1)).astype(BF16)
        )
        hidden_in.append(normed)
        value_bias = jnp.concatenate(
            [jnp.zeros((width,), F32), qv_bias[stream, 1].astype(F32)], axis=0
        )
        key_values.append(
            tall(stream, (dot(normed, kv_full[stream]) + value_bias).astype(BF16))
        )
        queries.append(
            tall(stream, (dot(normed, q_full[stream]) + qv_bias[stream, 0]).astype(BF16))
        )

    key_parts = []
    for slot in range(slot_count):
        parts = []
        for stream in range(2):
            if ctx_count == 2:
                other = swap(key_values[stream][slot], "ctx")
                bias = key_bias[stream][slot]
                parts.append(
                    (
                        key_values[stream],
                        lax.dynamic_index_in_dim(bias, ctx_index, 0, keepdims=False),
                        True,
                        stream,
                    )
                )
                parts.append(
                    (
                        other,
                        lax.dynamic_index_in_dim(bias, 1 - ctx_index, 0, keepdims=False),
                        False,
                        stream,
                    )
                )
            else:
                everyone = lax.all_gather(key_values[stream][slot], "ctx", axis=0, tiled=False)
                parts.append((flat(everyone), flat(key_bias[stream][slot]), False, stream))
        key_parts.append(parts)
    outs, logs = [], []
    for slot in range(slot_count):
        out_image, out_text, log_total = attend(slot, queries, key_parts[slot])
        outs.append((out_image, out_text))
        logs.append(log_total)
    attended = [jnp.concatenate([out[stream] for out in outs], axis=0) for stream in range(2)]

    att_values, middles, hidden_mid, pre_acts, activs = [], [], [], [], []
    for stream in range(2):
        att_value = (
            tall(stream, pair_sum(dot_nt(attended[stream], out_full[stream]), "tp"))
            + attn_out_bias[stream]
        )
        middle = inputs[stream] + mod_of(stream, 2) * att_value
        normed = flat(modulate(middle, mod_of(stream, 3), mod_of(stream, 4)).astype(BF16))
        pre_act = dot(normed, up_full[stream]) + mlp_up_bias[stream]
        att_values.append(att_value)
        middles.append(middle)
        hidden_mid.append(normed)
        pre_acts.append(pre_act)
        activs.append(gelu_tanh(pre_act).astype(BF16))

    grad_finals, grad_mlp_low, down_bias_grads, pre_lows, up_bias_grads = [], [], [], [], []
    for stream in range(2):
        grad_final = (
            cotangents[stream].astype(F32) * live_rows[stream] * own_weights[:, None, None]
        )
        grad_mlp = grad_final * mod_of(stream, 5)
        grad_finals.append(grad_final)
        down_bias_grads.append(jnp.sum(flat(grad_mlp), axis=0))
        grad_mlp_low.append(flat(grad_mlp.astype(BF16)))
        grad_act = dot(grad_mlp_low[stream], down_full[stream])
        pre_grad = jax.vjp(gelu_tanh, pre_acts[stream])[1](grad_act)[0]
        up_bias_grads.append(jnp.sum(pre_grad, axis=0))
        pre_lows.append(pre_grad.astype(BF16))
    hid2_sums = [
        tall(stream, pair_sum(dot_nt(pre_lows[stream], up_full[stream]), "tp"))
        for stream in range(2)
    ]
    down_grads = [
        reduce_rows(dot_tn(grad_mlp_low[stream], activs[stream])) for stream in range(2)
    ]
    up_grads = [reduce_rows(dot_tn(hidden_mid[stream], pre_lows[stream])) for stream in range(2)]

    finals, gate2_grads = [], []
    for stream in range(2):
        mlp_value = (
            tall(stream, pair_sum(dot_nt(activs[stream], down_full[stream]), "tp"))
            + mlp_down_bias[stream]
        )
        gate2_grads.append(jnp.sum(grad_finals[stream] * mlp_value, axis=1))
        final = (
            (middles[stream] + mod_of(stream, 5) * mlp_value)
            * live_rows[stream]
            * own_live[:, None, None]
        )
        finals.append(final.astype(BF16))

    grad_middles, mid_mod_grads, gate1_grads, out_bias_grads = [], [], [], []
    out_grads, grad_attended = [], []
    for stream in range(2):
        back, shift_grad, scale_grad = modulate_back(
            middles[stream], mod_of(stream, 4), hid2_sums[stream]
        )
        grad_middle = grad_finals[stream] + back
        grad_middles.append(grad_middle)
        mid_mod_grads.append((shift_grad, scale_grad))
        gate1_grads.append(jnp.sum(grad_middle * att_values[stream], axis=1))
        grad_att = grad_middle * mod_of(stream, 2)
        out_bias_grads.append(jnp.sum(flat(grad_att), axis=0))
        grad_att_low = flat(grad_att.astype(BF16))
        grad_attended.append(tall(stream, dot(grad_att_low, out_full[stream]).astype(BF16)))
        out_grads.append(reduce_rows(dot_tn(grad_att_low, attended[stream])))

    query_grads, pair_grads = ([], []), ([], [])
    bias_sums = 0.0
    for slot in range(slot_count):
        results = attend_back(
            slot, queries, outs[slot], grad_attended, logs[slot], key_parts[slot]
        )
        bias_sums = bias_sums + jnp.stack(
            [jnp.swapaxes(part, 0, 1).reshape(2, width) for part in results[2:4]], axis=1
        )
        for stream in range(2):
            query_grads[stream].append(results[stream])
            if ctx_count == 2:
                mine, given = results[4 + 2 * stream], results[5 + 2 * stream]
                total = mine.astype(F32) + swap(given, "ctx").astype(F32)
            else:
                total = lax.psum_scatter(
                    results[4 + stream], "ctx", scatter_dimension=1, tiled=True
                ).astype(F32)
            pair_grads[stream].append(
                jnp.concatenate([total[0].astype(BF16), total[1].astype(BF16)], axis=1)
            )

    input_grads, mod_rows, q_weight_grads, kv_weight_grads = [], [], [], []
    for stream in range(2):
        query_grad = jnp.concatenate(query_grads[stream], axis=0)
        pair_grad = jnp.concatenate(pair_grads[stream], axis=0)
        hid_sum = tall(
            stream,
            pair_sum(
                dot_nt(query_grad, q_full[stream]) + dot_nt(pair_grad, kv_full[stream]), "tp"
            ),
        )
        q_weight_grads.append(reduce_rows(dot_tn(hidden_in[stream], query_grad)))
        kv_weight_grads.append(reduce_rows(dot_tn(hidden_in[stream], pair_grad)))
        back, shift_grad, scale_grad = modulate_back(inputs[stream], mod_of(stream, 1), hid_sum)
        input_grads.append((grad_middles[stream] + back).astype(BF16))
        mod_rows.append(
            jnp.stack(
                [
                    shift_grad,
                    scale_grad,
                    gate1_grads[stream],
                    mid_mod_grads[stream][0],
                    mid_mod_grads[stream][1],
                    gate2_grads[stream],
                ],
                axis=1,
            )
        )

    mod_grads = jnp.stack(mod_rows, axis=1)
    mod_half_grads = lax.dynamic_slice_in_dim(mod_grads, tp_index * spans, spans, 2)
    pieces = (
        mod_half_grads,
        bias_sums,
        jnp.stack(up_bias_grads, axis=0),
        jnp.stack(out_bias_grads, axis=0),
        jnp.stack(down_bias_grads, axis=0),
    )
    row = ctx_sum(jnp.concatenate([piece.reshape(-1) for piece in pieces], axis=0))
    everyone = lax.all_gather(row[None].astype(BF16), FSDP, axis=0, tiled=True).astype(F32)
    ends = []
    base = 0
    for piece in pieces:
        ends.append(everyone[:, base : base + piece.size].reshape((-1,) + piece.shape))
        base += piece.size
    mod_all = ends[0].reshape(seq_count, 2, spans, D)
    qv_bias_grad, up_bias_grad, out_bias_grad, down_bias_grad = [
        jnp.sum(part, axis=0) for part in ends[1:]
    ]
    ada_bias_grad = jnp.sum(mod_all, axis=0).reshape(2, spans * D)
    mod_low = mod_all.astype(BF16)
    ada_weight_grad = jnp.einsum(
        "sd,stke->tdke", activated, mod_low, preferred_element_type=F32
    ).reshape(2, rows_local, spans * D)
    silu_part = jnp.einsum("stke,tdke->sd", mod_low, ada_local, preferred_element_type=F32)
    cond_grad = jax.vjp(jax.nn.silu, cond_float)[1](pair_sum(silu_part, "tp"))[0]
    qkv_grad = jnp.stack(
        [
            jnp.concatenate(
                [q_weight_grads[stream][:, None], kv_weight_grads[stream].reshape(-1, 2, width)],
                axis=1,
            )
            for stream in range(2)
        ],
        axis=0,
    )
    return (
        finals[0],
        finals[1][:, :cap_text],
        input_grads[0],
        input_grads[1][:, :cap_text],
        cond_grad,
        ada_weight_grad,
        ada_bias_grad,
        qkv_grad,
        qv_bias_grad,
        jnp.stack([part.T for part in out_grads], axis=0),
        out_bias_grad,
        jnp.stack(up_grads, axis=0),
        up_bias_grad,
        jnp.stack([part.T for part in down_grads], axis=0),
        down_bias_grad,
    )


def solution(mesh):
    fsdp, ctx, tp = (mesh.shape[name] for name in ("fsdp", "ctx", "tp"))
    split = Mesh(mesh.devices.reshape(fsdp // 2, 2, ctx, tp), ("z", "core", "ctx", "tp"))
    rows = P(FSDP, "ctx", None)
    inner = P(None, FSDP, "tp")
    outer = P(None, "tp", FSDP)
    return jax.shard_map(
        on_device,
        mesh=split,
        in_specs=(
            rows,
            rows,
            P(None, FSDP),
            rows,
            rows,
            P(FSDP, None),
            P(FSDP, None),
            P(),
            inner,
            P(None, "tp"),
            P(None, FSDP, None, "tp"),
            P(None, None, "tp"),
            outer,
            P(),
            inner,
            P(None, "tp"),
            outer,
            P(),
        ),
        out_specs=(
            rows,
            rows,
            rows,
            rows,
            P(None, FSDP),
            inner,
            P(None, "tp"),
            P(None, FSDP, None, "tp"),
            P(None, None, "tp"),
            outer,
            P(),
            inner,
            P(None, "tp"),
            outer,
            P(),
        ),
        check_vma=False,
    )
```

```python
import functools

import jax
import jax.numpy as jnp
from jax import lax
from jax.experimental import pallas as pl
from jax.experimental.pallas import tpu as pltpu
from jax.sharding import Mesh
from jax.sharding import PartitionSpec as P

D = 1536
HEAD = 64
LANES = 128
MB = 2
F32 = jnp.float32
BF16 = jnp.bfloat16
FSDP = ("z", "core")
PAIR = ((0, 1), (1, 0))
DEAD = -1e30
LIGHT = pl.CostEstimate(flops=1, bytes_accessed=1, transcendentals=0)


def swap(values, axis):
    return lax.ppermute(values, axis, PAIR)


def after(value, *others):
    return lax.optimization_barrier((value,) + others)[0] if others else value


def pair_sum(values, axis, *ready):
    mine = values.astype(BF16)
    other = swap(mine, axis)
    return after(mine, *ready).astype(F32) + other.astype(F32)


def ctx_sum(values, *ready):
    if lax.axis_size("ctx") == 2:
        return pair_sum(values, "ctx", *ready)
    return lax.psum(values.astype(BF16), "ctx").astype(F32)


def dot(left, right):
    return lax.dot_general(left, right, (((1,), (0,)), ((), ())), preferred_element_type=F32)


def dot_nt(left, right):
    return lax.dot_general(left, right, (((1,), (1,)), ((), ())), preferred_element_type=F32)


def dot_tn(left, right):
    return lax.dot_general(left, right, (((0,), (0,)), ((), ())), preferred_element_type=F32)


def gather_rows(shard):
    streams, rows = shard.shape[:2]
    if lax.axis_size("ctx") == 2:
        piece = lax.dynamic_index_in_dim(shard, lax.axis_index("ctx"), 0, keepdims=False)
        piece = piece.reshape(rows, -1)
        whole = lax.all_gather(piece, ("ctx",) + FSDP, axis=0, tiled=True)
        return whole.reshape(streams, -1, piece.shape[1])
    return lax.all_gather(shard.reshape(streams, rows, -1), FSDP, axis=1, tiled=True)


def scatter_rows(part):
    over = FSDP + ("ctx",) if lax.axis_size("ctx") == 2 else FSDP
    return lax.psum_scatter(part.astype(BF16), over, scatter_dimension=0, tiled=True)


def rotate(values, step):
    count = lax.axis_size("z")
    return lax.ppermute(values, "z", [(index, (index + step) % count) for index in range(count)])


def halves(values, axis_name, dim):
    index = lax.axis_index(axis_name)
    keep = lax.dynamic_index_in_dim(values, index, dim, keepdims=False)
    give = lax.dynamic_index_in_dim(values, 1 - index, dim, keepdims=False)
    return keep, give


def add_low(left, right):
    return (left.astype(F32) + right.astype(F32)).astype(BF16)


def core_step(terms, *ready):
    if lax.axis_size("ctx") != 2:
        return jnp.concatenate([scatter_rows(term) for term in terms], axis=-1)
    count = lax.axis_size("z")
    sums = []
    for term in terms:
        keep, give = halves(term.reshape(count, 2, -1, term.shape[1]), "core", 1)
        sums.append(add_low(after(keep, *ready), swap(give, "core")))
    return jnp.concatenate(sums, axis=-1)


def ctx_step(chip, *ready):
    if lax.axis_size("ctx") != 2:
        return chip
    count, rows, columns = chip.shape
    keep, give = halves(chip.reshape(count, 2, rows // 2, columns), "ctx", 1)
    return add_low(after(keep, *ready), swap(give, "ctx"))


def z_step(both, *ready):
    if lax.axis_size("ctx") != 2:
        return both
    count, z_index = lax.axis_size("z"), lax.axis_index("z")
    keep = lax.dynamic_index_in_dim(both, z_index, 0, keepdims=False)
    total = after(keep, *ready).astype(F32)
    for step in range(1, count):
        target = lax.rem(z_index + step, count)
        given = lax.dynamic_index_in_dim(both, target, 0, keepdims=False)
        total = total + rotate(given, step).astype(F32)
    return total.astype(BF16)


def end_step(mine, *ready):
    if lax.axis_size("ctx") != 2:
        return ctx_sum(mine)
    other = swap(mine, "ctx")
    mine = after(mine, *ready)
    first = lax.axis_index("ctx") == 0
    return jnp.concatenate(
        [jnp.where(first, mine, other), jnp.where(first, other, mine)], axis=0
    ).astype(F32)


def gather_groups(row):
    count = lax.axis_size("z")
    other = swap(row, "core")
    first = lax.axis_index("core") == 0
    chip = jnp.stack([jnp.where(first, row, other), jnp.where(first, other, row)], axis=0)
    rows = [chip] + [rotate(chip, step) for step in range(1, count)]
    ring = jnp.stack([rows[-place % count] for place in range(2 * count)], axis=0)
    start = lax.rem(count - lax.axis_index("z"), count)
    return lax.dynamic_slice_in_dim(ring, start, count, 0).reshape(2 * count, -1)


def scatter_groups(parts):
    z_count = lax.axis_size("z")
    z_index = lax.axis_index("z")
    split = parts.reshape((z_count, 2) + parts.shape[1:])
    keep, give = halves(split, "core", 1)
    chip = keep + swap(give, "core")
    total = lax.dynamic_index_in_dim(chip, z_index, 0, keepdims=False)
    for step in range(1, z_count):
        target = lax.rem(z_index + step, z_count)
        sent = lax.dynamic_index_in_dim(chip, target, 0, keepdims=False)
        total = total + rotate(sent, step)
    return total


def normalise(values):
    row_mean = jnp.mean(values, axis=-1, keepdims=True)
    centred = values - row_mean
    inverse = lax.rsqrt(jnp.mean(centred * centred, axis=-1, keepdims=True) + 1e-06)
    return centred * inverse, inverse


def modulate(values, shift, scale):
    return normalise(values)[0] * (1.0 + scale) + shift


def modulate_back(values, scale, grad):
    unit, inverse = normalise(values)
    unit_grad = grad * (1.0 + scale)
    first = jnp.mean(unit_grad, axis=-1, keepdims=True)
    second = jnp.mean(unit_grad * unit, axis=-1, keepdims=True)
    back = inverse * (unit_grad - first - unit * second)
    return back, jnp.sum(grad, axis=1), jnp.sum(grad * unit, axis=1)


def gelu_tanh(values):
    return jax.nn.gelu(values, approximate=True)


def masked_pair(image, text, stacked, scale):
    first = lax.broadcasted_iota(jnp.int32, (1, LANES), 1) < HEAD
    rows = image.shape[0]
    half = rows + text.shape[0]
    for head in range(2):
        kept = first if head == 0 else jnp.logical_not(first)
        base = head * half
        stacked[base : base + rows] = jnp.where(kept, image * scale, 0.0).astype(BF16)
        stacked[base + rows : base + half] = jnp.where(kept, text * scale, 0.0).astype(BF16)


def unstack(pair):
    first = lax.broadcasted_iota(jnp.int32, (1, LANES), 1) < HEAD
    turned = pair.T
    half = turned.shape[0] // 2
    return jnp.where(first, turned[:half], turned[half:])


def attend_kernel(parts, image_rows, *refs):
    query_image, query_text = refs[0], refs[1]
    key_refs = refs[2 : 2 + parts]
    value_refs = refs[2 + parts : 2 + 2 * parts]
    bias_refs = refs[2 + 2 * parts : 2 + 3 * parts]
    out_image, out_text, log_ref, queries, scores = refs[2 + 3 * parts :]
    masked_pair(
        query_image[...].astype(F32), query_text[...].astype(F32), queries, HEAD ** (-0.5)
    )
    stacked = queries[...]
    top = None
    base = 0
    for part in range(parts):
        rows = key_refs[part].shape[0]
        score = dot_nt(key_refs[part][...], stacked) + bias_refs[part][...]
        scores[base : base + rows] = score
        part_top = jnp.max(score, axis=0, keepdims=True)
        top = part_top if top is None else jnp.maximum(top, part_top)
        base += rows
    total = jnp.zeros_like(top)
    attended = jnp.zeros((LANES, stacked.shape[0]), F32)
    base = 0
    for part in range(parts):
        rows = key_refs[part].shape[0]
        exponent = jnp.exp(scores[base : base + rows] - top)
        total = total + jnp.sum(exponent, axis=0, keepdims=True)
        attended = attended + dot_tn(value_refs[part][...], exponent.astype(BF16))
        base += rows
    result = unstack(attended / total)
    out_image[...] = result[:image_rows].astype(BF16)
    out_text[...] = result[image_rows:].astype(BF16)
    log_ref[...] = top + jnp.log(total)


def attend_back_kernel(streams, image_rows, *refs):
    parts = len(streams)
    query_image, query_text, out_image, out_text, grad_image, grad_text, log_ref = refs[:7]
    key_refs = refs[7 : 7 + parts]
    value_refs = refs[7 + parts : 7 + 2 * parts]
    bias_refs = refs[7 + 2 * parts : 7 + 3 * parts]
    rest = refs[7 + 3 * parts :]
    query_grad_image, query_grad_text, query_sum, value_sum = rest[:4]
    pair_grads = rest[4 : 4 + parts]
    queries, grads, products = rest[4 + parts :]
    masked_pair(
        query_image[...].astype(F32), query_text[...].astype(F32), queries, HEAD ** (-0.5)
    )
    grad_rows_image, grad_rows_text = grad_image[...].astype(F32), grad_text[...].astype(F32)
    masked_pair(grad_rows_image, grad_rows_text, grads, 1.0)
    first = lax.broadcasted_iota(jnp.int32, (1, LANES), 1) < HEAD
    product_image = grad_rows_image * out_image[...].astype(F32)
    product_text = grad_rows_text * out_text[...].astype(F32)
    half = product_image.shape[0] + product_text.shape[0]
    for head in range(2):
        kept = first if head == 0 else jnp.logical_not(first)
        base = head * half
        products[base : base + image_rows] = jnp.where(kept, product_image, 0.0)
        products[base + image_rows : base + half] = jnp.where(kept, product_text, 0.0)
    inner = jnp.sum(products[...].T, axis=0, keepdims=True)
    stacked, grad_stacked = queries[...], grads[...]
    log_total = log_ref[...]
    query_grad = jnp.zeros((LANES, stacked.shape[0]), F32)
    value_totals = [jnp.zeros((1, LANES), F32) for _ in range(2)]
    for part in range(parts):
        keys, values = key_refs[part][...], value_refs[part][...]
        probs = jnp.exp(dot_nt(keys, stacked) + bias_refs[part][...] - log_total)
        grad_probs = dot_nt(values, grad_stacked)
        grad_scores = (probs * (grad_probs - inner)).astype(BF16)
        value_grad = dot(probs.astype(BF16), grad_stacked)
        pair_grads[part][1] = value_grad.astype(BF16)
        stream = streams[part]
        value_totals[stream] = value_totals[stream] + jnp.sum(value_grad, axis=0, keepdims=True)
        pair_grads[part][0] = dot(grad_scores, stacked).astype(BF16)
        query_grad = query_grad + dot_tn(keys, grad_scores)
    result = unstack(query_grad) * HEAD ** (-0.5)
    query_grad_image[...] = result[:image_rows].astype(BF16)
    query_grad_text[...] = result[image_rows:].astype(BF16)
    query_sum[0:1] = jnp.sum(result[:image_rows], axis=0, keepdims=True)
    query_sum[1:2] = jnp.sum(result[image_rows:], axis=0, keepdims=True)
    for stream in range(2):
        value_sum[stream : stream + 1] = value_totals[stream]


def weight_kernel(groups, *refs):
    result = refs[-1]

    def body(step, carry):
        columns = pl.ds(pl.multiple_of(step * 256, 256), 256)
        base = 0
        place = 0
        for count, width in groups:
            total = None
            for _ in range(count):
                term = dot_tn(refs[place][:, columns], refs[place + 1][...])
                total = term if total is None else total + term
                place += 2
            result[columns, base : base + width] = total.astype(BF16)
            base += width
        return carry

    lax.fori_loop(0, result.shape[0] // 256, body, 0)


def weight_terms(groups):
    flat_operands = [part for group in groups for pair in group for part in pair]
    shape = tuple((len(group), group[0][1].shape[1]) for group in groups)
    rows = flat_operands[0].shape[1]
    return pl.pallas_call(
        functools.partial(weight_kernel, shape),
        in_specs=[pl.BlockSpec(memory_space=pltpu.VMEM)] * len(flat_operands),
        out_specs=pl.BlockSpec(memory_space=pltpu.VMEM),
        out_shape=jax.ShapeDtypeStruct((rows, sum(part[1] for part in shape)), BF16),
        compiler_params=pltpu.CompilerParams(vmem_limit_bytes=52 * 1024 * 1024),
        cost_estimate=LIGHT,
        name="weight_terms",
    )(*flat_operands)


def unit_parts(values):
    row_mean = jnp.mean(values, axis=-1, keepdims=True)
    centred = values - row_mean
    inverse = lax.rsqrt(jnp.mean(centred * centred, axis=-1, keepdims=True) + 1e-06)
    return centred * inverse, inverse


def middle_kernel(mine, other, tokens, mods, bias, att_ref, middle_ref, hidden_ref):
    att = mine[...].astype(F32) + other[...].astype(F32) + bias[...]
    middle = tokens[...].astype(F32) + mods[2:3] * att
    att_ref[...] = att
    middle_ref[...] = middle
    unit, _ = unit_parts(middle)
    hidden_ref[...] = (unit * (1.0 + mods[4:5]) + mods[3:4]).astype(BF16)


def add_rows(sums, values):
    @pl.when(pl.program_id(1) == 0)
    def _():
        sums[...] = jnp.zeros_like(sums)

    for place, value in enumerate(values):
        sums[place : place + 1] += jnp.sum(value, axis=0, keepdims=True)


def norm_back(values, scale, grad):
    unit, inverse = unit_parts(values)
    unit_grad = grad * (1.0 + scale)
    first = jnp.mean(unit_grad, axis=-1, keepdims=True)
    second = jnp.mean(unit_grad * unit, axis=-1, keepdims=True)
    return inverse * (unit_grad - first - unit * second), grad * unit


def middle_back_kernel(
    mine, other, middle, att, final_grad, mods, middle_grad, att_grad, sums
):
    grad = mine[...].astype(F32) + other[...].astype(F32)
    back, scaled = norm_back(middle[...], mods[4:5], grad)
    total = final_grad[...] + back
    middle_grad[...] = total
    low = total * mods[2:3]
    att_grad[...] = low.astype(BF16)
    add_rows(sums, (grad, scaled, total * att[...], low))


def edge_back_kernel(mine, other, tokens, middle_grad, mods, input_grad, sums):
    grad = mine[...].astype(F32) + other[...].astype(F32)
    back, scaled = norm_back(tokens[...].astype(F32), mods[1:2], grad)
    input_grad[...] = (middle_grad[...] + back).astype(BF16)
    add_rows(sums, (grad, scaled))


def by_rows(kernel, name, rows_arrays, slot_arrays, shared, outputs, with_sums):
    slots, rows = rows_arrays[0].shape[:2]
    step = next(size for size in (96, 72, 48, 32, 16) if rows % size == 0)
    row_spec = pl.BlockSpec((None, step, D), lambda slot, block: (slot, block, 0))
    sums_spec = pl.BlockSpec((None, 8, D), lambda slot, block: (slot, 0, 0))
    out_specs = [row_spec] * len(outputs)
    out_shape = [jax.ShapeDtypeStruct((slots, rows, D), dtype) for dtype in outputs]
    if with_sums:
        out_specs.append(sums_spec)
        out_shape.append(jax.ShapeDtypeStruct((slots, 8, D), F32))
    return pl.pallas_call(
        kernel,
        grid=(slots, rows // step),
        in_specs=[row_spec] * len(rows_arrays)
        + [
            pl.BlockSpec((None, part.shape[1], D), lambda slot, block: (slot, 0, 0))
            for part in slot_arrays
        ]
        + [pl.BlockSpec((1, D), lambda slot, block: (0, 0)) for _ in shared],
        out_specs=out_specs,
        out_shape=out_shape,
        compiler_params=pltpu.CompilerParams(vmem_limit_bytes=40 * 1024 * 1024),
        cost_estimate=LIGHT,
        name=name,
    )(*rows_arrays, *slot_arrays, *shared)


def block_of(slot, rows, base=0):
    return pl.BlockSpec((None, rows, LANES), lambda pair: (slot, 0, base + pair))


def flat_block(rows, base=0):
    return pl.BlockSpec((rows, LANES), lambda pair: (0, base + pair))


def column_block(rows):
    return pl.BlockSpec((rows, 1), lambda pair: (0, 0))


def key_specs(slot, key_parts, pairs):
    keys, values, biases = [], [], []
    for rows_array, _, here, _ in key_parts:
        rows = rows_array.shape[-2]
        if here:
            keys.append(block_of(slot, rows, pairs))
            values.append(block_of(slot, rows, 2 * pairs))
        else:
            keys.append(flat_block(rows))
            values.append(flat_block(rows, pairs))
        biases.append(column_block(rows))
    return keys + values + biases


def key_operands(key_parts):
    arrays = [part[0] for part in key_parts]
    return arrays + arrays + [part[1] for part in key_parts]


def attend(slot, width, queries, key_parts):
    image, text = queries
    image_rows, text_rows = image.shape[1], text.shape[1]
    pairs = width // LANES
    stacked = 2 * (image_rows + text_rows)
    key_rows = sum(part[0].shape[-2] for part in key_parts)
    return pl.pallas_call(
        functools.partial(attend_kernel, len(key_parts), image_rows),
        grid=(pairs,),
        in_specs=[block_of(slot, image_rows), block_of(slot, text_rows)]
        + key_specs(slot, key_parts, pairs),
        out_specs=[
            flat_block(image_rows),
            flat_block(text_rows),
            pl.BlockSpec((None, 1, stacked), lambda pair: (pair, 0, 0)),
        ],
        out_shape=[
            jax.ShapeDtypeStruct((image_rows, width), BF16),
            jax.ShapeDtypeStruct((text_rows, width), BF16),
            jax.ShapeDtypeStruct((pairs, 1, stacked), F32),
        ],
        scratch_shapes=[
            pltpu.VMEM((stacked, LANES), BF16),
            pltpu.VMEM((key_rows, stacked), F32),
        ],
        compiler_params=pltpu.CompilerParams(vmem_limit_bytes=48 * 1024 * 1024),
        cost_estimate=LIGHT,
        name="attend",
    )(image, text, *key_operands(key_parts))


def attend_back(slot, width, queries, outs, grads, log_total, key_parts):
    image, text = queries
    image_rows, text_rows = image.shape[1], text.shape[1]
    pairs = width // LANES
    stacked = 2 * (image_rows + text_rows)
    key_rows = sum(part[0].shape[-2] for part in key_parts)
    part_rows = [part[0].shape[-2] for part in key_parts]
    row_blocks = [block_of(slot, image_rows), block_of(slot, text_rows)]
    sum_block = pl.BlockSpec((None, 2, LANES), lambda pair: (pair, 0, 0))
    sum_shape = jax.ShapeDtypeStruct((pairs, 2, LANES), F32)
    return pl.pallas_call(
        functools.partial(
            attend_back_kernel, tuple(part[3] for part in key_parts), image_rows
        ),
        grid=(pairs,),
        in_specs=row_blocks
        + [flat_block(image_rows), flat_block(text_rows)]
        + [flat_block(image_rows), block_of(slot, text_rows)]
        + [pl.BlockSpec((None, 1, stacked), lambda pair: (pair, 0, 0))]
        + key_specs(slot, key_parts, pairs),
        out_specs=[flat_block(image_rows), flat_block(text_rows), sum_block, sum_block]
        + [pl.BlockSpec((2, rows, LANES), lambda pair: (0, 0, pair)) for rows in part_rows],
        out_shape=[
            jax.ShapeDtypeStruct((image_rows, width), BF16),
            jax.ShapeDtypeStruct((text_rows, width), BF16),
            sum_shape,
            sum_shape,
        ]
        + [jax.ShapeDtypeStruct((2, rows, width), BF16) for rows in part_rows],
        scratch_shapes=[
            pltpu.VMEM((stacked, LANES), BF16),
            pltpu.VMEM((stacked, LANES), BF16),
            pltpu.VMEM((stacked, LANES), F32),
        ],
        compiler_params=pltpu.CompilerParams(vmem_limit_bytes=48 * 1024 * 1024),
        cost_estimate=LIGHT,
        name="attend_back",
    )(image, text, outs[0], outs[1], grads[0], grads[1], log_total, *key_operands(key_parts))


def on_device(
    image_tokens,
    text_tokens,
    cond_vector,
    image_cotangent,
    text_cotangent,
    image_counts,
    text_counts,
    seq_live,
    ada_weight,
    ada_bias,
    qkv_weight,
    qv_bias,
    attn_out_weight,
    attn_out_bias,
    mlp_up_weight,
    mlp_up_bias,
    mlp_down_weight,
    mlp_down_bias,
):
    slot_count = image_tokens.shape[0]
    per_batch = slot_count // MB
    seq_count = seq_live.shape[0]
    cap_image = image_tokens.shape[1]
    cap_text = text_tokens.shape[1]
    text_rows = -(-cap_text // 16) * 16
    extra = ((0, 0), (0, text_rows - cap_text), (0, 0))
    caps = (cap_image, text_rows)
    group_index = lax.axis_index("z") * 2 + lax.axis_index("core")
    ctx_count = lax.axis_size("ctx")
    ctx_index = lax.axis_index("ctx")
    tp_index = lax.axis_index("tp")
    spans = 6 // lax.axis_size("tp")
    rows_local = ada_weight.shape[1]
    width = qkv_weight.shape[3]

    qkv_full = gather_rows(qkv_weight)
    out_full = gather_rows(jnp.swapaxes(attn_out_weight, 1, 2))
    up_full = gather_rows(mlp_up_weight)
    down_full = gather_rows(jnp.swapaxes(mlp_down_weight, 1, 2))

    live_all = seq_live.astype(F32)
    batch_index = jnp.arange(seq_count, dtype=jnp.int32) % slot_count // per_batch
    marked = (batch_index[:, None] == jnp.arange(MB, dtype=jnp.int32)[None, :]).astype(
        F32
    ) * live_all[:, None]
    members = jnp.sum(marked, axis=0)
    shares = jnp.sum(live_all) / (MB * jnp.maximum(members, 1.0))
    seq_weights = jnp.sum(marked * shares[None, :], axis=1)
    own_weights = lax.dynamic_slice_in_dim(seq_weights, group_index * slot_count, slot_count)
    own_live = lax.dynamic_slice_in_dim(live_all, group_index * slot_count, slot_count)

    cond_float = cond_vector.astype(F32)
    activated = jax.nn.silu(cond_float).astype(BF16)
    ada_partial = jnp.einsum("sd,tdk->stk", activated, ada_weight, preferred_element_type=F32)
    mod_half = scatter_groups(
        ada_partial.reshape(seq_count // slot_count, slot_count, 2, spans * D)
    ) + ada_bias
    mod_other = swap(mod_half, "tp")
    modulation = jnp.where(
        tp_index == 0,
        jnp.concatenate([mod_half, mod_other], axis=2),
        jnp.concatenate([mod_other, mod_half], axis=2),
    ).reshape(slot_count, 2, 6, D)

    counts = (image_counts, text_counts)
    live_rows = []
    key_bias = []
    for stream in range(2):
        places = jnp.arange(caps[stream], dtype=jnp.int32)
        own_counts = lax.dynamic_slice_in_dim(counts[stream], ctx_index, 1, 1)
        live_rows.append((places[None, :] < own_counts).astype(F32)[:, :, None])
        key_bias.append(
            jnp.where(
                places[None, None, :, None] < counts[stream][:, :, None, None], 0.0, DEAD
            ).astype(F32)
        )
    tokens = (image_tokens, jnp.pad(text_tokens, extra))
    cotangents = (image_cotangent, jnp.pad(text_cotangent, extra))

    def mod_of(stream, which):
        return modulation[:, stream, which][:, None, :]

    def flat(values):
        return values.reshape(-1, values.shape[-1])

    def tall(stream, values):
        return values.reshape(slot_count, caps[stream], values.shape[-1])

    inputs = [part.astype(F32) for part in tokens]
    hidden_in, projected = [], []
    for stream in range(2):
        normed = flat(
            modulate(inputs[stream], mod_of(stream, 0), mod_of(stream, 1)).astype(BF16)
        )
        hidden_in.append(normed)
        both_bias = qv_bias[stream].astype(F32)
        bias = jnp.concatenate([both_bias[0], jnp.zeros((width,), F32), both_bias[1]], axis=0)
        projected.append(tall(stream, (dot(normed, qkv_full[stream]) + bias).astype(BF16)))

    key_parts = []
    for slot in range(slot_count):
        parts = []
        for stream in range(2):
            if ctx_count == 2:
                other = swap(projected[stream][slot, :, width:], "ctx")
                bias = key_bias[stream][slot]
                parts.append(
                    (
                        projected[stream],
                        lax.dynamic_index_in_dim(bias, ctx_index, 0, keepdims=False),
                        True,
                        stream,
                    )
                )
                parts.append(
                    (
                        other,
                        lax.dynamic_index_in_dim(bias, 1 - ctx_index, 0, keepdims=False),
                        False,
                        stream,
                    )
                )
            else:
                everyone = lax.all_gather(
                    projected[stream][slot, :, width:], "ctx", axis=0, tiled=False
                )
                parts.append((flat(everyone), flat(key_bias[stream][slot]), False, stream))
        key_parts.append(parts)
    slots = range(slot_count)
    text_unit = slot_count

    def unit_stream(unit):
        return 1 if unit == text_unit else 0

    def unit_of(unit, values):
        if unit == text_unit:
            return values[1]
        return values[0][unit : unit + 1]

    def unit_mod(unit, which):
        return unit_of(unit, [mod_of(0, which), mod_of(1, which)])

    def unit_rows(unit, values):
        return values.reshape(-1, caps[unit_stream(unit)], values.shape[-1])

    mods = [modulation[:, 0], modulation[:, 1]]
    units = range(slot_count + 1)
    outs, logs, attended = [], [], []
    att_values, middles, hidden_units = {}, {}, {}

    def middle_of(unit, *ready):
        stream = unit_stream(unit)
        mine = dot_nt(attended[unit], out_full[stream]).astype(BF16)
        other = swap(mine, "tp")
        att_values[unit], middles[unit], hidden = by_rows(
            middle_kernel,
            "middle",
            [unit_rows(unit, after(mine, *ready)), unit_rows(unit, other), unit_of(unit, tokens)],
            [unit_of(unit, mods)],
            [attn_out_bias[stream].astype(F32)[None]],
            [F32, F32, BF16],
            False,
        )
        hidden_units[unit] = flat(hidden)

    ready = ()
    for slot in slots:
        out_image, out_text, log_total = attend(
            slot,
            width,
            [after(part, *ready) for part in projected],
            key_parts[slot],
        )
        outs.append((out_image, out_text))
        logs.append(log_total)
        attended.append(out_image)
        if slot == slot_count - 1:
            attended.append(jnp.concatenate([out[1] for out in outs], axis=0))
            middle_of(text_unit)
        middle_of(slot)
        ready = (hidden_units[slot],)
    hidden_mid = [
        jnp.concatenate([hidden_units[slot] for slot in slots], axis=0),
        hidden_units[text_unit],
    ]
    pre_acts = [dot(hidden_mid[stream], up_full[stream]) + mlp_up_bias[stream] for stream in range(2)]
    activs = [gelu_tanh(pre_act).astype(BF16) for pre_act in pre_acts]

    grad_finals, grad_mlp_low, down_bias_grads = [], [], []
    for stream in range(2):
        grad_final = (
            cotangents[stream].astype(F32) * live_rows[stream] * own_weights[:, None, None]
        )
        grad_mlp = grad_final * mod_of(stream, 5)
        grad_finals.append(grad_final)
        down_bias_grads.append(jnp.sum(flat(grad_mlp), axis=0))
        grad_mlp_low.append(flat(grad_mlp.astype(BF16)))
    def mlp_weight_term(stream, *ready):
        return dot_tn(after(grad_mlp_low[stream], *ready), activs[stream]).astype(BF16)

    def up_weight_term(stream, *ready):
        return dot_tn(after(hidden_mid[stream], *ready), pre_lows[stream]).astype(BF16)

    down_terms = [mlp_weight_term(0, activs[1])]
    down_terms.append(mlp_weight_term(1, down_terms[0]))
    pre_lows, up_bias_grads, hid2_parts = [None, None], [None, None], {}
    up_terms = [None, None]
    ready = tuple(down_terms)
    for stream in (1, 0):
        grad_act = dot(after(grad_mlp_low[stream], *ready), down_full[stream])
        pre_grad = jax.vjp(gelu_tanh, pre_acts[stream])[1](grad_act)[0]
        up_bias_grads[stream] = jnp.sum(pre_grad, axis=0)
        pre_lows[stream] = pre_grad.astype(BF16)
        for unit in units:
            if unit_stream(unit) != stream:
                continue
            rows = pre_lows[stream]
            if stream == 0:
                rows = rows[unit * cap_image : (unit + 1) * cap_image]
            hid2_parts[unit] = dot_nt(after(rows, *ready), up_full[stream]).astype(BF16)
            ready = (hid2_parts[unit],)
        if stream == 0:
            up_chip = core_step([up_terms[1]], *ready)
            ready = (up_chip,)
        up_terms[stream] = up_weight_term(stream, *ready)
        ready = (up_terms[stream],)
    down_shards = [scatter_rows(term) for term in down_terms]
    up_shard = scatter_rows(after(up_terms[0], down_terms[1]))

    grad_middles, mid_sums, grad_att_low, grad_attended = {}, {}, {}, {}

    def middle_back(unit, *ready):
        stream = unit_stream(unit)
        other = swap(hid2_parts[unit], "tp")
        grad_middles[unit], low, mid_sums[unit] = by_rows(
            middle_back_kernel,
            "middle_back",
            [
                unit_rows(unit, after(hid2_parts[unit], *ready)),
                unit_rows(unit, other),
                middles[unit],
                att_values[unit],
                unit_of(unit, grad_finals),
            ],
            [unit_of(unit, mods)],
            [],
            [F32, BF16],
            True,
        )
        grad_att_low[unit] = flat(low)
        grad_attended[unit] = dot(grad_att_low[unit], out_full[stream]).astype(BF16)

    query_grads, given_pairs = {}, {}
    bias_sums = 0.0
    mlp_parts = []
    for slot in slots:
        middle_back(slot, *ready)
        if slot == 0:
            middle_back(text_unit, grad_attended[slot])
            ready = (grad_attended[text_unit],)
        results = attend_back(
            slot,
            width,
            projected,
            outs[slot],
            (
                after(grad_attended[slot], *ready),
                tall(1, grad_attended[text_unit]),
            ),
            logs[slot],
            key_parts[slot],
        )
        ready = (results[0],)
        bias_sums = bias_sums + jnp.stack(
            [jnp.swapaxes(part, 0, 1).reshape(2, width) for part in results[2:4]], axis=1
        )
        for stream in range(2):
            query_grads[slot, stream] = results[stream]
            if ctx_count == 2:
                given_pairs[slot, stream] = (
                    results[4 + 2 * stream],
                    swap(results[5 + 2 * stream], "ctx"),
                )
            else:
                total = lax.psum_scatter(
                    results[4 + stream], "ctx", scatter_dimension=1, tiled=True
                )
                given_pairs[slot, stream] = (total, jnp.zeros_like(total))
        if slot == 0:
            up_both = ctx_step(up_chip, *ready)
            for stream in range(2):
                rows = after(activs[stream], up_both, *ready)
                mlp_parts.append(dot_nt(rows, down_full[stream]).astype(BF16))
                ready = (mlp_parts[stream],)

    pair_grads, hid_parts = {}, {}

    def hid_part(slot, *ready):
        for stream in range(2):
            mine, given = given_pairs[slot, stream]
            total = add_low(after(mine, *ready), given)
            pair_grads[slot, stream] = jnp.concatenate([total[0], total[1]], axis=1)
        rows = jnp.concatenate([query_grads[slot, 0], pair_grads[slot, 0]], axis=1)
        hid_parts[slot] = dot_nt(rows, qkv_full[0]).astype(BF16)

    hid_part(0, *ready)
    ready = (hid_parts[0],)
    finals, gate2_grads = [], []
    for stream in range(2):
        mlp_value = (
            tall(stream, pair_sum(mlp_parts[stream], "tp", *ready)) + mlp_down_bias[stream]
        )
        gate2_grads.append(jnp.sum(grad_finals[stream] * mlp_value, axis=1))
        middle = middles[text_unit]
        if stream == 0:
            middle = jnp.concatenate([middles[slot] for slot in slots], axis=0)
        final = (
            (middle + mod_of(stream, 5) * mlp_value)
            * live_rows[stream]
            * own_live[:, None, None]
        )
        finals.append(final.astype(BF16))
    ready = tuple(finals)
    groups = []
    for stream in range(2):
        members = list(slots) if stream == 0 else [text_unit]
        groups.append([(after(grad_att_low[unit], *ready), attended[unit]) for unit in members])
    for stream in range(2):
        normed = tall(stream, hidden_in[stream])
        groups.append([(normed[slot], query_grads[slot, stream]) for slot in slots])
    first_term = weight_terms(groups)
    first_shard = scatter_rows(first_term)
    ready = (first_term,)
    for slot in slots[1:]:
        hid_part(slot, *ready)
        ready = (hid_parts[slot],)
    text_rows_grad = jnp.concatenate(
        [
            jnp.concatenate([query_grads[slot, 1], pair_grads[slot, 1]], axis=1)
            for slot in slots
        ],
        axis=0,
    )
    hid_parts[text_unit] = dot_nt(after(text_rows_grad, *ready), qkv_full[1]).astype(BF16)
    ready = (hid_parts[text_unit],)
    groups = []
    for stream in range(2):
        normed = tall(stream, hidden_in[stream])
        groups.append(
            [(after(normed[slot], *ready), pair_grads[slot, stream]) for slot in slots]
        )
    second_term = weight_terms(groups)
    second_shard = scatter_rows(second_term)
    ready = (second_term,)
    input_grads, edge_sums = {}, {}
    for unit in list(slots) + [text_unit]:
        other = swap(hid_parts[unit], "tp")
        input_grads[unit], edge_sums[unit] = by_rows(
            edge_back_kernel,
            "edge_back",
            [
                unit_rows(unit, after(hid_parts[unit], *ready)),
                unit_rows(unit, other),
                unit_of(unit, tokens),
                grad_middles[unit],
            ],
            [unit_of(unit, mods)],
            [],
            [BF16],
            True,
        )
        ready = (input_grads[unit],)
    up_mine = z_step(up_both, *ready)
    down_grads = [end_step(shard, *ready) for shard in down_shards]
    up_grads = [end_step(up_shard, *ready), end_step(up_mine)]
    first_grads = end_step(first_shard)
    second_grads = end_step(second_shard)
    out_grads = [first_grads[:, :width], first_grads[:, width : 2 * width]]
    q_weight_grads = [first_grads[:, 2 * width : 3 * width], first_grads[:, 3 * width :]]
    kv_weight_grads = [second_grads[:, : 2 * width], second_grads[:, 2 * width :]]

    def by_slot(values):
        image = jnp.concatenate([values[slot] for slot in slots], axis=0)
        return jnp.stack([image, values[text_unit]], axis=1)

    mod_grads = jnp.stack(
        [
            by_slot({unit: edge_sums[unit][:, 0] for unit in units}),
            by_slot({unit: edge_sums[unit][:, 1] for unit in units}),
            by_slot({unit: mid_sums[unit][:, 2] for unit in units}),
            by_slot({unit: mid_sums[unit][:, 0] for unit in units}),
            by_slot({unit: mid_sums[unit][:, 1] for unit in units}),
            jnp.stack(gate2_grads, axis=1),
        ],
        axis=2,
    )
    out_bias_sums = [
        sum(mid_sums[slot][0, 3] for slot in slots),
        jnp.sum(mid_sums[text_unit][:, 3], axis=0),
    ]
    input_grads = [
        jnp.concatenate([input_grads[slot] for slot in slots], axis=0),
        input_grads[text_unit],
    ]

    mod_half_grads = lax.dynamic_slice_in_dim(mod_grads, tp_index * spans, spans, 2)
    pieces = (
        mod_half_grads,
        bias_sums,
        jnp.stack(up_bias_grads, axis=0),
        jnp.stack(out_bias_sums, axis=0),
        jnp.stack(down_bias_grads, axis=0),
    )
    row = ctx_sum(jnp.concatenate([piece.reshape(-1) for piece in pieces], axis=0))
    everyone = gather_groups(row.astype(BF16)).astype(F32)
    ends = []
    base = 0
    for piece in pieces:
        ends.append(everyone[:, base : base + piece.size].reshape((-1,) + piece.shape))
        base += piece.size
    mod_all = ends[0].reshape(seq_count, 2, spans * D)
    qv_bias_grad, up_bias_grad, out_bias_grad, down_bias_grad = [
        jnp.sum(part, axis=0) for part in ends[1:]
    ]
    ada_bias_grad = jnp.sum(mod_all, axis=0)
    mod_low = mod_all.astype(BF16)
    ada_weight_grad = jnp.einsum(
        "sd,stk->tdk", activated, mod_low, preferred_element_type=F32
    )
    silu_part = jnp.einsum("stk,tdk->sd", mod_low, ada_weight, preferred_element_type=F32)
    cond_grad = jax.vjp(jax.nn.silu, cond_float)[1](pair_sum(silu_part, "tp"))[0]
    qkv_grad = jnp.stack(
        [
            jnp.concatenate(
                [q_weight_grads[stream][:, None], kv_weight_grads[stream].reshape(-1, 2, width)],
                axis=1,
            )
            for stream in range(2)
        ],
        axis=0,
    )
    return (
        finals[0],
        finals[1][:, :cap_text],
        input_grads[0],
        input_grads[1][:, :cap_text],
        cond_grad,
        ada_weight_grad,
        ada_bias_grad,
        qkv_grad,
        qv_bias_grad,
        jnp.stack([part.T for part in out_grads], axis=0),
        out_bias_grad,
        jnp.stack(up_grads, axis=0),
        up_bias_grad,
        jnp.stack([part.T for part in down_grads], axis=0),
        down_bias_grad,
    )


def solution(mesh):
    fsdp, ctx, tp = (mesh.shape[name] for name in ("fsdp", "ctx", "tp"))
    split = Mesh(mesh.devices.reshape(fsdp // 2, 2, ctx, tp), ("z", "core", "ctx", "tp"))
    rows = P(FSDP, "ctx", None)
    inner = P(None, FSDP, "tp")
    outer = P(None, "tp", FSDP)
    return jax.shard_map(
        on_device,
        mesh=split,
        in_specs=(
            rows,
            rows,
            P(None, FSDP),
            rows,
            rows,
            P(FSDP, None),
            P(FSDP, None),
            P(),
            inner,
            P(None, "tp"),
            P(None, FSDP, None, "tp"),
            P(None, None, "tp"),
            outer,
            P(),
            inner,
            P(None, "tp"),
            outer,
            P(),
        ),
        out_specs=(
            rows,
            rows,
            rows,
            rows,
            P(None, FSDP),
            inner,
            P(None, "tp"),
            P(None, FSDP, None, "tp"),
            P(None, None, "tp"),
            outer,
            P(),
            inner,
            P(None, "tp"),
            outer,
            P(),
        ),
        check_vma=False,
    )
```

```python
import functools

import jax
import jax.numpy as jnp
from jax import lax
from jax.experimental import pallas as pl
from jax.experimental.pallas import tpu as pltpu
from jax.sharding import Mesh
from jax.sharding import PartitionSpec as P

D = 1536
HEAD = 64
LANES = 128
MB = 2
F32 = jnp.float32
BF16 = jnp.bfloat16
FSDP = ("z", "core")
PAIR = ((0, 1), (1, 0))
DEAD = -1e30
LIGHT = pl.CostEstimate(flops=1, bytes_accessed=1, transcendentals=0)


def swap(values, axis):
    return lax.ppermute(values, axis, PAIR)


def after(value, *others):
    return lax.optimization_barrier((value,) + others)[0] if others else value


def pair_sum(values, axis, *ready):
    mine = values.astype(BF16)
    other = swap(mine, axis)
    return after(mine, *ready).astype(F32) + other.astype(F32)


def ctx_sum(values, *ready):
    if lax.axis_size("ctx") == 2:
        return pair_sum(values, "ctx", *ready)
    return lax.psum(values.astype(BF16), "ctx").astype(F32)


def dot(left, right):
    return lax.dot_general(left, right, (((1,), (0,)), ((), ())), preferred_element_type=F32)


def dot_nt(left, right):
    return lax.dot_general(left, right, (((1,), (1,)), ((), ())), preferred_element_type=F32)


def dot_tn(left, right):
    return lax.dot_general(left, right, (((0,), (0,)), ((), ())), preferred_element_type=F32)


def gather_rows(shard):
    streams, rows = shard.shape[:2]
    if lax.axis_size("ctx") == 2:
        piece = lax.dynamic_index_in_dim(shard, lax.axis_index("ctx"), 0, keepdims=False)
        piece = piece.reshape(rows, -1)
        whole = lax.all_gather(piece, ("ctx",) + FSDP, axis=0, tiled=True)
        return whole.reshape(streams, -1, piece.shape[1])
    return lax.all_gather(shard.reshape(streams, rows, -1), FSDP, axis=1, tiled=True)


def gather_over_fsdp(shard):
    pair = jnp.concatenate([shard[0], shard[1]], axis=1)
    whole = lax.all_gather(pair, FSDP, axis=0, tiled=True)
    columns = shard.shape[2]
    return whole[:, :columns], whole[:, columns:]


def scatter_rows(part):
    return lax.psum_scatter(part.astype(BF16), FSDP, scatter_dimension=0, tiled=True)


def rotate(values, step):
    count = lax.axis_size("z")
    return lax.ppermute(values, "z", [(index, (index + step) % count) for index in range(count)])


def halves(values, axis_name, dim):
    index = lax.axis_index(axis_name)
    keep = lax.dynamic_index_in_dim(values, index, dim, keepdims=False)
    give = lax.dynamic_index_in_dim(values, 1 - index, dim, keepdims=False)
    return keep, give


def add_low(left, right):
    return (left.astype(F32) + right.astype(F32)).astype(BF16)


def core_step(terms, *ready):
    if lax.axis_size("ctx") != 2:
        return jnp.concatenate([scatter_rows(term) for term in terms], axis=-1)
    count = lax.axis_size("z")
    sums = []
    for term in terms:
        keep, give = halves(term.reshape(count, 2, -1, term.shape[1]), "core", 1)
        sums.append(add_low(after(keep, *ready), swap(give, "core")))
    return jnp.concatenate(sums, axis=-1)


def ctx_step(chip, *ready):
    if lax.axis_size("ctx") != 2:
        return chip
    count, rows, columns = chip.shape
    keep, give = halves(chip.reshape(count, 2, rows // 2, columns), "ctx", 1)
    return add_low(after(keep, *ready), swap(give, "ctx"))


def z_step(both):
    if lax.axis_size("ctx") != 2:
        return both
    return lax.psum_scatter(
        both.reshape(-1, both.shape[2]), "z", scatter_dimension=0, tiled=True
    )


def ctx_given(mine):
    if lax.axis_size("ctx") == 2:
        return swap(mine, "ctx")
    return lax.psum(mine, "ctx")


def ctx_total(mine, given):
    if lax.axis_size("ctx") == 2:
        return mine.astype(F32) + given.astype(F32)
    return given.astype(F32)


def end_step(mine, *ready):
    if lax.axis_size("ctx") != 2:
        return ctx_sum(mine)
    other = swap(mine, "ctx")
    mine = after(mine, *ready)
    first = lax.axis_index("ctx") == 0
    return jnp.concatenate(
        [jnp.where(first, mine, other), jnp.where(first, other, mine)], axis=0
    ).astype(F32)


def gather_groups(row):
    count = lax.axis_size("z")
    other = swap(row, "core")
    first = lax.axis_index("core") == 0
    chip = jnp.stack([jnp.where(first, row, other), jnp.where(first, other, row)], axis=0)
    rows = [chip] + [rotate(chip, step) for step in range(1, count)]
    ring = jnp.stack([rows[-place % count] for place in range(2 * count)], axis=0)
    start = lax.rem(count - lax.axis_index("z"), count)
    return lax.dynamic_slice_in_dim(ring, start, count, 0).reshape(2 * count, -1)


def scatter_groups(parts):
    z_count = lax.axis_size("z")
    z_index = lax.axis_index("z")
    split = parts.reshape((z_count, 2) + parts.shape[1:])
    keep, give = halves(split, "core", 1)
    chip = keep + swap(give, "core")
    total = lax.dynamic_index_in_dim(chip, z_index, 0, keepdims=False)
    for step in range(1, z_count):
        target = lax.rem(z_index + step, z_count)
        sent = lax.dynamic_index_in_dim(chip, target, 0, keepdims=False)
        total = total + rotate(sent, step)
    return total


def normalise(values):
    row_mean = jnp.mean(values, axis=-1, keepdims=True)
    centred = values - row_mean
    inverse = lax.rsqrt(jnp.mean(centred * centred, axis=-1, keepdims=True) + 1e-06)
    return centred * inverse, inverse


def modulate(values, shift, scale):
    return normalise(values)[0] * (1.0 + scale) + shift


def modulate_back(values, scale, grad):
    unit, inverse = normalise(values)
    unit_grad = grad * (1.0 + scale)
    first = jnp.mean(unit_grad, axis=-1, keepdims=True)
    second = jnp.mean(unit_grad * unit, axis=-1, keepdims=True)
    back = inverse * (unit_grad - first - unit * second)
    return back, jnp.sum(grad, axis=1), jnp.sum(grad * unit, axis=1)


def gelu_tanh(values):
    return jax.nn.gelu(values, approximate=True)


def masked_pair(image, text, stacked, scale):
    first = lax.broadcasted_iota(jnp.int32, (1, LANES), 1) < HEAD
    rows = image.shape[0]
    half = rows + text.shape[0]
    for head in range(2):
        kept = first if head == 0 else jnp.logical_not(first)
        base = head * half
        stacked[base : base + rows] = jnp.where(kept, image * scale, 0.0).astype(BF16)
        stacked[base + rows : base + half] = jnp.where(kept, text * scale, 0.0).astype(BF16)


def unstack(pair):
    first = lax.broadcasted_iota(jnp.int32, (1, LANES), 1) < HEAD
    turned = pair.T
    half = turned.shape[0] // 2
    return jnp.where(first, turned[:half], turned[half:])


def attend_kernel(parts, image_rows, *refs):
    query_image, query_text = refs[0], refs[1]
    key_refs = refs[2 : 2 + parts]
    value_refs = refs[2 + parts : 2 + 2 * parts]
    bias_refs = refs[2 + 2 * parts : 2 + 3 * parts]
    out_image, out_text, log_ref, queries, scores = refs[2 + 3 * parts :]
    masked_pair(
        query_image[...].astype(F32), query_text[...].astype(F32), queries, HEAD ** (-0.5)
    )
    stacked = queries[...]
    top = None
    base = 0
    for part in range(parts):
        rows = key_refs[part].shape[0]
        score = dot_nt(key_refs[part][...], stacked) + bias_refs[part][...]
        scores[base : base + rows] = score
        part_top = jnp.max(score, axis=0, keepdims=True)
        top = part_top if top is None else jnp.maximum(top, part_top)
        base += rows
    total = jnp.zeros_like(top)
    attended = jnp.zeros((LANES, stacked.shape[0]), F32)
    base = 0
    for part in range(parts):
        rows = key_refs[part].shape[0]
        exponent = jnp.exp(scores[base : base + rows] - top)
        total = total + jnp.sum(exponent, axis=0, keepdims=True)
        attended = attended + dot_tn(value_refs[part][...], exponent.astype(BF16))
        base += rows
    result = unstack(attended / total)
    out_image[...] = result[:image_rows].astype(BF16)
    out_text[...] = result[image_rows:].astype(BF16)
    log_ref[...] = top + jnp.log(total)


def attend_back_kernel(streams, image_rows, *refs):
    parts = len(streams)
    query_image, query_text, out_image, out_text, grad_image, grad_text, log_ref = refs[:7]
    key_refs = refs[7 : 7 + parts]
    value_refs = refs[7 + parts : 7 + 2 * parts]
    bias_refs = refs[7 + 2 * parts : 7 + 3 * parts]
    rest = refs[7 + 3 * parts :]
    query_grad_image, query_grad_text, query_sum, value_sum = rest[:4]
    pair_grads = rest[4 : 4 + parts]
    queries, grads, products = rest[4 + parts :]
    masked_pair(
        query_image[...].astype(F32), query_text[...].astype(F32), queries, HEAD ** (-0.5)
    )
    grad_rows_image, grad_rows_text = grad_image[...].astype(F32), grad_text[...].astype(F32)
    masked_pair(grad_rows_image, grad_rows_text, grads, 1.0)
    first = lax.broadcasted_iota(jnp.int32, (1, LANES), 1) < HEAD
    product_image = grad_rows_image * out_image[...].astype(F32)
    product_text = grad_rows_text * out_text[...].astype(F32)
    half = product_image.shape[0] + product_text.shape[0]
    for head in range(2):
        kept = first if head == 0 else jnp.logical_not(first)
        base = head * half
        products[base : base + image_rows] = jnp.where(kept, product_image, 0.0)
        products[base + image_rows : base + half] = jnp.where(kept, product_text, 0.0)
    inner = jnp.sum(products[...].T, axis=0, keepdims=True)
    stacked, grad_stacked = queries[...], grads[...]
    log_total = log_ref[...]
    query_grad = jnp.zeros((LANES, stacked.shape[0]), F32)
    value_totals = [jnp.zeros((1, LANES), F32) for _ in range(2)]
    for part in range(parts):
        keys, values = key_refs[part][...], value_refs[part][...]
        probs = jnp.exp(dot_nt(keys, stacked) + bias_refs[part][...] - log_total)
        grad_probs = dot_nt(values, grad_stacked)
        grad_scores = (probs * (grad_probs - inner)).astype(BF16)
        value_grad = dot(probs.astype(BF16), grad_stacked)
        pair_grads[part][1] = value_grad.astype(BF16)
        stream = streams[part]
        value_totals[stream] = value_totals[stream] + jnp.sum(value_grad, axis=0, keepdims=True)
        pair_grads[part][0] = dot(grad_scores, stacked).astype(BF16)
        query_grad = query_grad + dot_tn(keys, grad_scores)
    result = unstack(query_grad) * HEAD ** (-0.5)
    query_grad_image[...] = result[:image_rows].astype(BF16)
    query_grad_text[...] = result[image_rows:].astype(BF16)
    query_sum[0:1] = jnp.sum(result[:image_rows], axis=0, keepdims=True)
    query_sum[1:2] = jnp.sum(result[image_rows:], axis=0, keepdims=True)
    for stream in range(2):
        value_sum[stream : stream + 1] = value_totals[stream]


def weight_kernel(groups, *refs):
    result = refs[-1]

    def body(step, carry):
        columns = pl.ds(pl.multiple_of(step * 256, 256), 256)
        base = 0
        place = 0
        for count, width in groups:
            total = None
            for _ in range(count):
                term = dot_tn(refs[place][:, columns], refs[place + 1][...])
                total = term if total is None else total + term
                place += 2
            result[columns, base : base + width] = total.astype(BF16)
            base += width
        return carry

    lax.fori_loop(0, result.shape[0] // 256, body, 0)


def weight_terms(groups):
    flat_operands = [part for group in groups for pair in group for part in pair]
    shape = tuple((len(group), group[0][1].shape[1]) for group in groups)
    rows = flat_operands[0].shape[1]
    return pl.pallas_call(
        functools.partial(weight_kernel, shape),
        in_specs=[pl.BlockSpec(memory_space=pltpu.VMEM)] * len(flat_operands),
        out_specs=pl.BlockSpec(memory_space=pltpu.VMEM),
        out_shape=jax.ShapeDtypeStruct((rows, sum(part[1] for part in shape)), BF16),
        compiler_params=pltpu.CompilerParams(vmem_limit_bytes=52 * 1024 * 1024),
        cost_estimate=LIGHT,
        name="weight_terms",
    )(*flat_operands)


def unit_parts(values):
    row_mean = jnp.mean(values, axis=-1, keepdims=True)
    centred = values - row_mean
    inverse = lax.rsqrt(jnp.mean(centred * centred, axis=-1, keepdims=True) + 1e-06)
    return centred * inverse, inverse


def middle_kernel(mine, other, tokens, mods, bias, att_ref, middle_ref, hidden_ref):
    att = mine[...].astype(F32) + other[...].astype(F32) + bias[...]
    middle = tokens[...].astype(F32) + mods[2:3] * att
    att_ref[...] = att
    middle_ref[...] = middle
    unit, _ = unit_parts(middle)
    hidden_ref[...] = (unit * (1.0 + mods[4:5]) + mods[3:4]).astype(BF16)


def add_rows(sums, values):
    @pl.when(pl.program_id(1) == 0)
    def _():
        sums[...] = jnp.zeros_like(sums)

    for place, value in enumerate(values):
        sums[place : place + 1] += jnp.sum(value, axis=0, keepdims=True)


def norm_back(values, scale, grad):
    unit, inverse = unit_parts(values)
    unit_grad = grad * (1.0 + scale)
    first = jnp.mean(unit_grad, axis=-1, keepdims=True)
    second = jnp.mean(unit_grad * unit, axis=-1, keepdims=True)
    return inverse * (unit_grad - first - unit * second), grad * unit


def middle_back_kernel(
    mine, other, middle, att, final_grad, mods, middle_grad, att_grad, sums
):
    grad = mine[...].astype(F32) + other[...].astype(F32)
    back, scaled = norm_back(middle[...], mods[4:5], grad)
    total = final_grad[...] + back
    middle_grad[...] = total
    low = total * mods[2:3]
    att_grad[...] = low.astype(BF16)
    add_rows(sums, (grad, scaled, total * att[...], low))


def edge_back_kernel(mine, other, tokens, middle_grad, mods, input_grad, sums):
    grad = mine[...].astype(F32) + other[...].astype(F32)
    back, scaled = norm_back(tokens[...].astype(F32), mods[1:2], grad)
    input_grad[...] = (middle_grad[...] + back).astype(BF16)
    add_rows(sums, (grad, scaled))


def by_rows(kernel, name, rows_arrays, slot_arrays, shared, outputs, with_sums):
    slots, rows = rows_arrays[0].shape[:2]
    step = next(size for size in (96, 72, 48, 32, 16) if rows % size == 0)
    row_spec = pl.BlockSpec((None, step, D), lambda slot, block: (slot, block, 0))
    sums_spec = pl.BlockSpec((None, 8, D), lambda slot, block: (slot, 0, 0))
    out_specs = [row_spec] * len(outputs)
    out_shape = [jax.ShapeDtypeStruct((slots, rows, D), dtype) for dtype in outputs]
    if with_sums:
        out_specs.append(sums_spec)
        out_shape.append(jax.ShapeDtypeStruct((slots, 8, D), F32))
    return pl.pallas_call(
        kernel,
        grid=(slots, rows // step),
        in_specs=[row_spec] * len(rows_arrays)
        + [
            pl.BlockSpec((None, part.shape[1], D), lambda slot, block: (slot, 0, 0))
            for part in slot_arrays
        ]
        + [pl.BlockSpec((1, D), lambda slot, block: (0, 0)) for _ in shared],
        out_specs=out_specs,
        out_shape=out_shape,
        compiler_params=pltpu.CompilerParams(vmem_limit_bytes=40 * 1024 * 1024),
        cost_estimate=LIGHT,
        name=name,
    )(*rows_arrays, *slot_arrays, *shared)


def block_of(slot, rows, base=0):
    return pl.BlockSpec((None, rows, LANES), lambda pair: (slot, 0, base + pair))


def flat_block(rows, base=0):
    return pl.BlockSpec((rows, LANES), lambda pair: (0, base + pair))


def column_block(rows):
    return pl.BlockSpec((rows, 1), lambda pair: (0, 0))


def key_specs(slot, key_parts, pairs):
    keys, values, biases = [], [], []
    for rows_array, _, here, _ in key_parts:
        rows = rows_array.shape[-2]
        if here:
            keys.append(block_of(slot, rows, pairs))
            values.append(block_of(slot, rows, 2 * pairs))
        else:
            keys.append(flat_block(rows))
            values.append(flat_block(rows, pairs))
        biases.append(column_block(rows))
    return keys + values + biases


def key_operands(key_parts):
    arrays = [part[0] for part in key_parts]
    return arrays + arrays + [part[1] for part in key_parts]


def attend(slot, width, queries, key_parts):
    image, text = queries
    image_rows, text_rows = image.shape[1], text.shape[1]
    pairs = width // LANES
    stacked = 2 * (image_rows + text_rows)
    key_rows = sum(part[0].shape[-2] for part in key_parts)
    return pl.pallas_call(
        functools.partial(attend_kernel, len(key_parts), image_rows),
        grid=(pairs,),
        in_specs=[block_of(slot, image_rows), block_of(slot, text_rows)]
        + key_specs(slot, key_parts, pairs),
        out_specs=[
            flat_block(image_rows),
            flat_block(text_rows),
            pl.BlockSpec((None, 1, stacked), lambda pair: (pair, 0, 0)),
        ],
        out_shape=[
            jax.ShapeDtypeStruct((image_rows, width), BF16),
            jax.ShapeDtypeStruct((text_rows, width), BF16),
            jax.ShapeDtypeStruct((pairs, 1, stacked), F32),
        ],
        scratch_shapes=[
            pltpu.VMEM((stacked, LANES), BF16),
            pltpu.VMEM((key_rows, stacked), F32),
        ],
        compiler_params=pltpu.CompilerParams(vmem_limit_bytes=48 * 1024 * 1024),
        cost_estimate=LIGHT,
        name="attend",
    )(image, text, *key_operands(key_parts))


def attend_back(slot, width, queries, outs, grads, log_total, key_parts):
    image, text = queries
    image_rows, text_rows = image.shape[1], text.shape[1]
    pairs = width // LANES
    stacked = 2 * (image_rows + text_rows)
    key_rows = sum(part[0].shape[-2] for part in key_parts)
    part_rows = [part[0].shape[-2] for part in key_parts]
    row_blocks = [block_of(slot, image_rows), block_of(slot, text_rows)]
    sum_block = pl.BlockSpec((None, 2, LANES), lambda pair: (pair, 0, 0))
    sum_shape = jax.ShapeDtypeStruct((pairs, 2, LANES), F32)
    return pl.pallas_call(
        functools.partial(
            attend_back_kernel, tuple(part[3] for part in key_parts), image_rows
        ),
        grid=(pairs,),
        in_specs=row_blocks
        + [flat_block(image_rows), flat_block(text_rows)]
        + [flat_block(image_rows), block_of(slot, text_rows)]
        + [pl.BlockSpec((None, 1, stacked), lambda pair: (pair, 0, 0))]
        + key_specs(slot, key_parts, pairs),
        out_specs=[flat_block(image_rows), flat_block(text_rows), sum_block, sum_block]
        + [pl.BlockSpec((2, rows, LANES), lambda pair: (0, 0, pair)) for rows in part_rows],
        out_shape=[
            jax.ShapeDtypeStruct((image_rows, width), BF16),
            jax.ShapeDtypeStruct((text_rows, width), BF16),
            sum_shape,
            sum_shape,
        ]
        + [jax.ShapeDtypeStruct((2, rows, width), BF16) for rows in part_rows],
        scratch_shapes=[
            pltpu.VMEM((stacked, LANES), BF16),
            pltpu.VMEM((stacked, LANES), BF16),
            pltpu.VMEM((stacked, LANES), F32),
        ],
        compiler_params=pltpu.CompilerParams(vmem_limit_bytes=48 * 1024 * 1024),
        cost_estimate=LIGHT,
        name="attend_back",
    )(image, text, outs[0], outs[1], grads[0], grads[1], log_total, *key_operands(key_parts))


def on_device(
    image_tokens,
    text_tokens,
    cond_vector,
    image_cotangent,
    text_cotangent,
    image_counts,
    text_counts,
    seq_live,
    ada_weight,
    ada_bias,
    qkv_weight,
    qv_bias,
    attn_out_weight,
    attn_out_bias,
    mlp_up_weight,
    mlp_up_bias,
    mlp_down_weight,
    mlp_down_bias,
):
    slot_count = image_tokens.shape[0]
    per_batch = slot_count // MB
    seq_count = seq_live.shape[0]
    cap_image = image_tokens.shape[1]
    cap_text = text_tokens.shape[1]
    text_rows = -(-cap_text // 16) * 16
    extra = ((0, 0), (0, text_rows - cap_text), (0, 0))
    caps = (cap_image, text_rows)
    group_index = lax.axis_index("z") * 2 + lax.axis_index("core")
    ctx_count = lax.axis_size("ctx")
    ctx_index = lax.axis_index("ctx")
    tp_index = lax.axis_index("tp")
    spans = 6 // lax.axis_size("tp")
    rows_local = ada_weight.shape[1]
    width = qkv_weight.shape[3]

    qkv_full = gather_rows(qkv_weight)
    out_full = gather_over_fsdp(jnp.swapaxes(attn_out_weight, 1, 2))
    up_full = gather_rows(mlp_up_weight)
    down_full = gather_rows(jnp.swapaxes(mlp_down_weight, 1, 2))

    live_all = seq_live.astype(F32)
    batch_index = jnp.arange(seq_count, dtype=jnp.int32) % slot_count // per_batch
    marked = (batch_index[:, None] == jnp.arange(MB, dtype=jnp.int32)[None, :]).astype(
        F32
    ) * live_all[:, None]
    members = jnp.sum(marked, axis=0)
    shares = jnp.sum(live_all) / (MB * jnp.maximum(members, 1.0))
    seq_weights = jnp.sum(marked * shares[None, :], axis=1)
    own_weights = lax.dynamic_slice_in_dim(seq_weights, group_index * slot_count, slot_count)
    own_live = lax.dynamic_slice_in_dim(live_all, group_index * slot_count, slot_count)

    cond_float = cond_vector.astype(F32)
    activated = jax.nn.silu(cond_float).astype(BF16)
    ada_partial = jnp.einsum("sd,tdk->stk", activated, ada_weight, preferred_element_type=F32)
    mod_half = scatter_groups(
        ada_partial.reshape(seq_count // slot_count, slot_count, 2, spans * D)
    ) + ada_bias
    mod_other = swap(mod_half, "tp")
    modulation = jnp.where(
        tp_index == 0,
        jnp.concatenate([mod_half, mod_other], axis=2),
        jnp.concatenate([mod_other, mod_half], axis=2),
    ).reshape(slot_count, 2, 6, D)

    counts = (image_counts, text_counts)
    live_rows = []
    key_bias = []
    for stream in range(2):
        places = jnp.arange(caps[stream], dtype=jnp.int32)
        own_counts = lax.dynamic_slice_in_dim(counts[stream], ctx_index, 1, 1)
        live_rows.append((places[None, :] < own_counts).astype(F32)[:, :, None])
        key_bias.append(
            jnp.where(
                places[None, None, :, None] < counts[stream][:, :, None, None], 0.0, DEAD
            ).astype(F32)
        )
    tokens = (image_tokens, jnp.pad(text_tokens, extra))
    cotangents = (image_cotangent, jnp.pad(text_cotangent, extra))

    def mod_of(stream, which):
        return modulation[:, stream, which][:, None, :]

    def flat(values):
        return values.reshape(-1, values.shape[-1])

    def tall(stream, values):
        return values.reshape(slot_count, caps[stream], values.shape[-1])

    inputs = [part.astype(F32) for part in tokens]
    hidden_in, projected = [], []
    for stream in range(2):
        normed = flat(
            modulate(inputs[stream], mod_of(stream, 0), mod_of(stream, 1)).astype(BF16)
        )
        hidden_in.append(normed)
        both_bias = qv_bias[stream].astype(F32)
        bias = jnp.concatenate([both_bias[0], jnp.zeros((width,), F32), both_bias[1]], axis=0)
        projected.append(tall(stream, (dot(normed, qkv_full[stream]) + bias).astype(BF16)))

    key_parts = []
    for slot in range(slot_count):
        parts = []
        for stream in range(2):
            if ctx_count == 2:
                other = swap(projected[stream][slot, :, width:], "ctx")
                bias = key_bias[stream][slot]
                parts.append(
                    (
                        projected[stream],
                        lax.dynamic_index_in_dim(bias, ctx_index, 0, keepdims=False),
                        True,
                        stream,
                    )
                )
                parts.append(
                    (
                        other,
                        lax.dynamic_index_in_dim(bias, 1 - ctx_index, 0, keepdims=False),
                        False,
                        stream,
                    )
                )
            else:
                everyone = lax.all_gather(
                    projected[stream][slot, :, width:], "ctx", axis=0, tiled=False
                )
                parts.append((flat(everyone), flat(key_bias[stream][slot]), False, stream))
        key_parts.append(parts)
    slots = range(slot_count)
    text_unit = slot_count

    def unit_stream(unit):
        return 1 if unit == text_unit else 0

    def unit_of(unit, values):
        if unit == text_unit:
            return values[1]
        return values[0][unit : unit + 1]

    def unit_mod(unit, which):
        return unit_of(unit, [mod_of(0, which), mod_of(1, which)])

    def unit_rows(unit, values):
        return values.reshape(-1, caps[unit_stream(unit)], values.shape[-1])

    mods = [modulation[:, 0], modulation[:, 1]]
    units = range(slot_count + 1)
    outs, logs, attended = [], [], []
    att_values, middles, hidden_units = {}, {}, {}

    def middle_of(unit, *ready):
        stream = unit_stream(unit)
        mine = dot_nt(attended[unit], out_full[stream]).astype(BF16)
        other = swap(mine, "tp")
        att_values[unit], middles[unit], hidden = by_rows(
            middle_kernel,
            "middle",
            [unit_rows(unit, after(mine, *ready)), unit_rows(unit, other), unit_of(unit, tokens)],
            [unit_of(unit, mods)],
            [attn_out_bias[stream].astype(F32)[None]],
            [F32, F32, BF16],
            False,
        )
        hidden_units[unit] = flat(hidden)

    ready = ()
    for slot in slots:
        out_image, out_text, log_total = attend(
            slot,
            width,
            [after(part, *ready) for part in projected],
            key_parts[slot],
        )
        outs.append((out_image, out_text))
        logs.append(log_total)
        attended.append(out_image)
        if slot == slot_count - 1:
            attended.append(jnp.concatenate([out[1] for out in outs], axis=0))
            middle_of(text_unit)
        middle_of(slot)
        ready = (hidden_units[slot],)
    hidden_mid = [
        jnp.concatenate([hidden_units[slot] for slot in slots], axis=0),
        hidden_units[text_unit],
    ]
    pre_acts = [dot(hidden_mid[stream], up_full[stream]) + mlp_up_bias[stream] for stream in range(2)]
    activs = [gelu_tanh(pre_act).astype(BF16) for pre_act in pre_acts]

    grad_finals, grad_mlp_low, down_bias_grads = [], [], []
    for stream in range(2):
        grad_final = (
            cotangents[stream].astype(F32) * live_rows[stream] * own_weights[:, None, None]
        )
        grad_mlp = grad_final * mod_of(stream, 5)
        grad_finals.append(grad_final)
        down_bias_grads.append(jnp.sum(flat(grad_mlp), axis=0))
        grad_mlp_low.append(flat(grad_mlp.astype(BF16)))
    def mlp_weight_term(stream, *ready):
        return dot_tn(after(grad_mlp_low[stream], *ready), activs[stream]).astype(BF16)

    def up_weight_term(stream, *ready):
        return dot_tn(after(hidden_mid[stream], *ready), pre_lows[stream]).astype(BF16)

    down_terms = [mlp_weight_term(0, activs[1])]
    down_terms.append(mlp_weight_term(1, down_terms[0]))
    pre_lows, up_bias_grads, hid2_parts = [None, None], [None, None], {}
    up_terms = [None, None]
    ready = tuple(down_terms)
    for stream in (1, 0):
        grad_act = dot(after(grad_mlp_low[stream], *ready), down_full[stream])
        pre_grad = jax.vjp(gelu_tanh, pre_acts[stream])[1](grad_act)[0]
        up_bias_grads[stream] = jnp.sum(pre_grad, axis=0)
        pre_lows[stream] = pre_grad.astype(BF16)
        for unit in units:
            if unit_stream(unit) != stream:
                continue
            rows = pre_lows[stream]
            if stream == 0:
                rows = rows[unit * cap_image : (unit + 1) * cap_image]
            hid2_parts[unit] = dot_nt(after(rows, *ready), up_full[stream]).astype(BF16)
            ready = (hid2_parts[unit],)
        if stream == 0:
            up_chip = core_step([up_terms[1]], *ready)
            ready = (up_chip,)
        else:
            up_terms[stream] = up_weight_term(stream, *ready)
            ready = (up_terms[stream],)
    down_shards = [scatter_rows(term) for term in down_terms]

    grad_middles, mid_sums, grad_att_low, grad_attended = {}, {}, {}, {}

    def middle_back(unit, *ready):
        stream = unit_stream(unit)
        other = swap(hid2_parts[unit], "tp")
        grad_middles[unit], low, mid_sums[unit] = by_rows(
            middle_back_kernel,
            "middle_back",
            [
                unit_rows(unit, after(hid2_parts[unit], *ready)),
                unit_rows(unit, other),
                middles[unit],
                att_values[unit],
                unit_of(unit, grad_finals),
            ],
            [unit_of(unit, mods)],
            [],
            [F32, BF16],
            True,
        )
        grad_att_low[unit] = flat(low)
        grad_attended[unit] = dot(grad_att_low[unit], out_full[stream]).astype(BF16)

    query_grads, given_pairs = {}, {}
    bias_sums = 0.0
    mlp_parts = []
    for slot in slots:
        middle_back(slot, *ready, *down_shards[slot : slot + 1])
        if slot == 0:
            middle_back(text_unit, grad_attended[slot])
            ready = (grad_attended[text_unit],)
        results = attend_back(
            slot,
            width,
            projected,
            outs[slot],
            (
                after(grad_attended[slot], *ready),
                tall(1, grad_attended[text_unit]),
            ),
            logs[slot],
            key_parts[slot],
        )
        ready = (results[0],)
        bias_sums = bias_sums + jnp.stack(
            [jnp.swapaxes(part, 0, 1).reshape(2, width) for part in results[2:4]], axis=1
        )
        for stream in range(2):
            query_grads[slot, stream] = results[stream]
            if ctx_count == 2:
                given_pairs[slot, stream] = (
                    results[4 + 2 * stream],
                    swap(results[5 + 2 * stream], "ctx"),
                )
            else:
                total = lax.psum_scatter(
                    results[4 + stream], "ctx", scatter_dimension=1, tiled=True
                )
                given_pairs[slot, stream] = (total, jnp.zeros_like(total))
        if slot == 0:
            up_terms[0] = up_weight_term(0, *ready)
            up_shard = scatter_rows(up_terms[0])
            ready = (up_terms[0],)
            for stream in range(2):
                rows = after(activs[stream], *ready)
                mlp_parts.append(dot_nt(rows, down_full[stream]).astype(BF16))
                ready = (mlp_parts[stream],)
            up_both = ctx_step(up_chip, *ready)

    pair_grads, hid_parts = {}, {}

    def hid_part(slot, *ready):
        for stream in range(2):
            mine, given = given_pairs[slot, stream]
            total = add_low(after(mine, *ready), given)
            pair_grads[slot, stream] = jnp.concatenate([total[0], total[1]], axis=1)
        rows = jnp.concatenate([query_grads[slot, 0], pair_grads[slot, 0]], axis=1)
        hid_parts[slot] = dot_nt(rows, qkv_full[0]).astype(BF16)

    hid_part(0, *ready)
    ready = (hid_parts[0],)
    finals, gate2_grads = [], []
    for stream in range(2):
        mlp_value = (
            tall(stream, pair_sum(mlp_parts[stream], "tp", *ready)) + mlp_down_bias[stream]
        )
        gate2_grads.append(jnp.sum(grad_finals[stream] * mlp_value, axis=1))
        middle = middles[text_unit]
        if stream == 0:
            middle = jnp.concatenate([middles[slot] for slot in slots], axis=0)
        final = (
            (middle + mod_of(stream, 5) * mlp_value)
            * live_rows[stream]
            * own_live[:, None, None]
        )
        finals.append(final.astype(BF16))
    ready = tuple(finals)
    for slot in slots[1:]:
        hid_part(slot, *ready)
        ready = (hid_parts[slot],)
    groups = []
    for stream in range(2):
        members = list(slots) if stream == 0 else [text_unit]
        groups.append(
            [(after(grad_att_low[unit], *ready, up_shard), attended[unit]) for unit in members]
        )
    for stream in range(2):
        normed = tall(stream, hidden_in[stream])
        groups.append([(normed[slot], query_grads[slot, stream]) for slot in slots])
    first_term = weight_terms(groups)
    first_shard = scatter_rows(first_term)
    ready = (first_term,)
    text_rows_grad = jnp.concatenate(
        [
            jnp.concatenate([query_grads[slot, 1], pair_grads[slot, 1]], axis=1)
            for slot in slots
        ],
        axis=0,
    )
    hid_parts[text_unit] = dot_nt(after(text_rows_grad, *ready), qkv_full[1]).astype(BF16)
    ready = (hid_parts[text_unit],)
    groups = []
    for stream in range(2):
        normed = tall(stream, hidden_in[stream])
        groups.append(
            [(after(normed[slot], *ready), pair_grads[slot, stream]) for slot in slots]
        )
    second_term = weight_terms(groups)
    second_shard = scatter_rows(second_term)
    up_mine = z_step(up_both)
    down_given = [ctx_given(after(shard, second_term)) for shard in down_shards]
    up_given = ctx_given(after(up_shard, second_term))
    ready = (second_term, up_mine, up_given, down_given[0])
    input_grads, edge_sums = {}, {}
    for unit in list(slots) + [text_unit]:
        other = swap(hid_parts[unit], "tp")
        input_grads[unit], edge_sums[unit] = by_rows(
            edge_back_kernel,
            "edge_back",
            [
                unit_rows(unit, after(hid_parts[unit], *ready)),
                unit_rows(unit, other),
                unit_of(unit, tokens),
                grad_middles[unit],
            ],
            [unit_of(unit, mods)],
            [],
            [BF16],
            True,
        )
        ready = (input_grads[unit], down_given[1])
    first_given = ctx_given(first_shard)
    down_grads = [ctx_total(*pair) for pair in zip(down_shards, down_given)]
    up_grads = [ctx_total(up_shard, up_given), end_step(up_mine)]
    first_grads = ctx_total(first_shard, first_given)
    def by_slot(values):
        image = jnp.concatenate([values[slot] for slot in slots], axis=0)
        return jnp.stack([image, values[text_unit]], axis=1)

    mod_grads = jnp.stack(
        [
            by_slot({unit: edge_sums[unit][:, 0] for unit in units}),
            by_slot({unit: edge_sums[unit][:, 1] for unit in units}),
            by_slot({unit: mid_sums[unit][:, 2] for unit in units}),
            by_slot({unit: mid_sums[unit][:, 0] for unit in units}),
            by_slot({unit: mid_sums[unit][:, 1] for unit in units}),
            jnp.stack(gate2_grads, axis=1),
        ],
        axis=2,
    )
    out_bias_sums = [
        sum(mid_sums[slot][0, 3] for slot in slots),
        jnp.sum(mid_sums[text_unit][:, 3], axis=0),
    ]
    input_grads = [
        jnp.concatenate([input_grads[slot] for slot in slots], axis=0),
        input_grads[text_unit],
    ]

    mod_half_grads = lax.dynamic_slice_in_dim(mod_grads, tp_index * spans, spans, 2)
    pieces = (
        mod_half_grads,
        bias_sums,
        jnp.stack(up_bias_grads, axis=0),
        jnp.stack(out_bias_sums, axis=0),
        jnp.stack(down_bias_grads, axis=0),
    )
    row = jnp.concatenate([piece.reshape(-1) for piece in pieces], axis=0).astype(BF16)
    row = ctx_sum(row)
    gathered = gather_groups(after(row.astype(BF16), first_shard))
    second_shard = after(second_shard, gathered)
    second_grads = ctx_total(second_shard, ctx_given(second_shard))
    out_grads = [first_grads[:, :width], first_grads[:, width : 2 * width]]
    q_weight_grads = [first_grads[:, 2 * width : 3 * width], first_grads[:, 3 * width :]]
    kv_weight_grads = [second_grads[:, : 2 * width], second_grads[:, 2 * width :]]
    everyone = gathered.astype(F32)
    ends = []
    base = 0
    for piece in pieces:
        ends.append(everyone[:, base : base + piece.size].reshape((-1,) + piece.shape))
        base += piece.size
    mod_all = ends[0].reshape(seq_count, 2, spans * D)
    qv_bias_grad, up_bias_grad, out_bias_grad, down_bias_grad = [
        jnp.sum(part, axis=0) for part in ends[1:]
    ]
    ada_bias_grad = jnp.sum(mod_all, axis=0)
    mod_low = mod_all.astype(BF16)
    ada_weight_grad = jnp.einsum(
        "sd,stk->tdk", activated, mod_low, preferred_element_type=F32
    )
    silu_part = jnp.einsum("stk,tdk->sd", mod_low, ada_weight, preferred_element_type=F32)
    cond_grad = jax.vjp(jax.nn.silu, cond_float)[1](pair_sum(silu_part, "tp"))[0]
    qkv_grad = jnp.stack(
        [
            jnp.concatenate(
                [q_weight_grads[stream][:, None], kv_weight_grads[stream].reshape(-1, 2, width)],
                axis=1,
            )
            for stream in range(2)
        ],
        axis=0,
    )
    return (
        finals[0],
        finals[1][:, :cap_text],
        input_grads[0],
        input_grads[1][:, :cap_text],
        cond_grad,
        ada_weight_grad,
        ada_bias_grad,
        qkv_grad,
        qv_bias_grad,
        jnp.stack([part.T for part in out_grads], axis=0),
        out_bias_grad,
        jnp.stack(up_grads, axis=0),
        up_bias_grad,
        jnp.stack([part.T for part in down_grads], axis=0),
        down_bias_grad,
    )


def solution(mesh):
    fsdp, ctx, tp = (mesh.shape[name] for name in ("fsdp", "ctx", "tp"))
    split = Mesh(mesh.devices.reshape(fsdp // 2, 2, ctx, tp), ("z", "core", "ctx", "tp"))
    rows = P(FSDP, "ctx", None)
    inner = P(None, FSDP, "tp")
    outer = P(None, "tp", FSDP)
    return jax.shard_map(
        on_device,
        mesh=split,
        in_specs=(
            rows,
            rows,
            P(None, FSDP),
            rows,
            rows,
            P(FSDP, None),
            P(FSDP, None),
            P(),
            inner,
            P(None, "tp"),
            P(None, FSDP, None, "tp"),
            P(None, None, "tp"),
            outer,
            P(),
            inner,
            P(None, "tp"),
            outer,
            P(),
        ),
        out_specs=(
            rows,
            rows,
            rows,
            rows,
            P(None, FSDP),
            inner,
            P(None, "tp"),
            P(None, FSDP, None, "tp"),
            P(None, None, "tp"),
            outer,
            P(),
            inner,
            P(None, "tp"),
            outer,
            P(),
        ),
        check_vma=False,
    )
```

```python
import functools

import jax
import jax.numpy as jnp
from jax import lax
from jax.experimental import pallas as pl
from jax.experimental.pallas import tpu as pltpu
from jax.sharding import Mesh
from jax.sharding import PartitionSpec as P

D = 1536
HEAD = 64
LANES = 128
MB = 2
F32 = jnp.float32
BF16 = jnp.bfloat16
FSDP = ("z", "core")
PAIR = ((0, 1), (1, 0))
DEAD = -1e30
LIGHT = pl.CostEstimate(flops=1, bytes_accessed=1, transcendentals=0)


def swap(values, axis):
    return lax.ppermute(values, axis, PAIR)


def after(value, *others):
    return lax.optimization_barrier((value,) + others)[0] if others else value


def pair_sum(values, axis, *ready):
    mine = values.astype(BF16)
    other = swap(mine, axis)
    return after(mine, *ready).astype(F32) + other.astype(F32)


def ctx_sum(values, *ready):
    if lax.axis_size("ctx") == 2:
        return pair_sum(values, "ctx", *ready)
    return lax.psum(values.astype(BF16), "ctx").astype(F32)


def dot(left, right):
    return lax.dot_general(left, right, (((1,), (0,)), ((), ())), preferred_element_type=F32)


def dot_nt(left, right):
    return lax.dot_general(left, right, (((1,), (1,)), ((), ())), preferred_element_type=F32)


def dot_tn(left, right):
    return lax.dot_general(left, right, (((0,), (0,)), ((), ())), preferred_element_type=F32)


def gather_rows(shard):
    streams, rows = shard.shape[:2]
    if lax.axis_size("ctx") == 2:
        piece = lax.dynamic_index_in_dim(shard, lax.axis_index("ctx"), 0, keepdims=False)
        piece = piece.reshape(rows, -1)
        whole = lax.all_gather(piece, ("ctx",) + FSDP, axis=0, tiled=True)
        return whole.reshape(streams, -1, piece.shape[1])
    return lax.all_gather(shard.reshape(streams, rows, -1), FSDP, axis=1, tiled=True)


def gather_over_fsdp(shard):
    pair = jnp.concatenate([shard[0], shard[1]], axis=1)
    whole = lax.all_gather(pair, FSDP, axis=0, tiled=True)
    columns = shard.shape[2]
    return whole[:, :columns], whole[:, columns:]


def scatter_rows(part):
    return lax.psum_scatter(part.astype(BF16), FSDP, scatter_dimension=0, tiled=True)


def rotate(values, step):
    count = lax.axis_size("z")
    return lax.ppermute(values, "z", [(index, (index + step) % count) for index in range(count)])


def halves(values, axis_name, dim):
    index = lax.axis_index(axis_name)
    keep = lax.dynamic_index_in_dim(values, index, dim, keepdims=False)
    give = lax.dynamic_index_in_dim(values, 1 - index, dim, keepdims=False)
    return keep, give


def add_low(left, right):
    return (left.astype(F32) + right.astype(F32)).astype(BF16)


def core_step(terms, *ready):
    if lax.axis_size("ctx") != 2:
        return jnp.concatenate([scatter_rows(term) for term in terms], axis=-1)
    count = lax.axis_size("z")
    sums = []
    for term in terms:
        keep, give = halves(term.reshape(count, 2, -1, term.shape[1]), "core", 1)
        sums.append(add_low(after(keep, *ready), swap(give, "core")))
    return jnp.concatenate(sums, axis=-1)


def ctx_step(chip, *ready):
    if lax.axis_size("ctx") != 2:
        return chip
    count, rows, columns = chip.shape
    keep, give = halves(chip.reshape(count, 2, rows // 2, columns), "ctx", 1)
    return add_low(after(keep, *ready), swap(give, "ctx"))


def z_step(both):
    if lax.axis_size("ctx") != 2:
        return both
    return lax.psum_scatter(
        both.reshape(-1, both.shape[2]), "z", scatter_dimension=0, tiled=True
    )


def ctx_given(mine):
    if lax.axis_size("ctx") == 2:
        return swap(mine, "ctx")
    return lax.psum(mine, "ctx")


def ctx_total(mine, given):
    if lax.axis_size("ctx") == 2:
        return mine.astype(F32) + given.astype(F32)
    return given.astype(F32)


def end_step(mine, *ready):
    if lax.axis_size("ctx") != 2:
        return ctx_sum(mine)
    other = swap(mine, "ctx")
    mine = after(mine, *ready)
    first = lax.axis_index("ctx") == 0
    return jnp.concatenate(
        [jnp.where(first, mine, other), jnp.where(first, other, mine)], axis=0
    ).astype(F32)


def gather_groups(row):
    count = lax.axis_size("z")
    other = swap(row, "core")
    first = lax.axis_index("core") == 0
    chip = jnp.stack([jnp.where(first, row, other), jnp.where(first, other, row)], axis=0)
    rows = [chip] + [rotate(chip, step) for step in range(1, count)]
    ring = jnp.stack([rows[-place % count] for place in range(2 * count)], axis=0)
    start = lax.rem(count - lax.axis_index("z"), count)
    return lax.dynamic_slice_in_dim(ring, start, count, 0).reshape(2 * count, -1)


def scatter_groups(parts):
    z_count = lax.axis_size("z")
    z_index = lax.axis_index("z")
    split = parts.reshape((z_count, 2) + parts.shape[1:])
    keep, give = halves(split, "core", 1)
    chip = keep + swap(give, "core")
    total = lax.dynamic_index_in_dim(chip, z_index, 0, keepdims=False)
    for step in range(1, z_count):
        target = lax.rem(z_index + step, z_count)
        sent = lax.dynamic_index_in_dim(chip, target, 0, keepdims=False)
        total = total + rotate(sent, step)
    return total


def normalise(values):
    row_mean = jnp.mean(values, axis=-1, keepdims=True)
    centred = values - row_mean
    inverse = lax.rsqrt(jnp.mean(centred * centred, axis=-1, keepdims=True) + 1e-06)
    return centred * inverse, inverse


def modulate(values, shift, scale):
    return normalise(values)[0] * (1.0 + scale) + shift


def modulate_back(values, scale, grad):
    unit, inverse = normalise(values)
    unit_grad = grad * (1.0 + scale)
    first = jnp.mean(unit_grad, axis=-1, keepdims=True)
    second = jnp.mean(unit_grad * unit, axis=-1, keepdims=True)
    back = inverse * (unit_grad - first - unit * second)
    return back, jnp.sum(grad, axis=1), jnp.sum(grad * unit, axis=1)


def gelu_tanh(values):
    return jax.nn.gelu(values, approximate=True)


def masked_pair(image, text, stacked, scale):
    first = lax.broadcasted_iota(jnp.int32, (1, LANES), 1) < HEAD
    rows = image.shape[0]
    half = rows + text.shape[0]
    for head in range(2):
        kept = first if head == 0 else jnp.logical_not(first)
        base = head * half
        stacked[base : base + rows] = jnp.where(kept, image * scale, 0.0).astype(BF16)
        stacked[base + rows : base + half] = jnp.where(kept, text * scale, 0.0).astype(BF16)


def unstack(pair):
    first = lax.broadcasted_iota(jnp.int32, (1, LANES), 1) < HEAD
    turned = pair.T
    half = turned.shape[0] // 2
    return jnp.where(first, turned[:half], turned[half:])


def attend_kernel(parts, image_rows, *refs):
    query_image, query_text = refs[0], refs[1]
    key_refs = refs[2 : 2 + parts]
    value_refs = refs[2 + parts : 2 + 2 * parts]
    bias_refs = refs[2 + 2 * parts : 2 + 3 * parts]
    out_image, out_text, log_ref, queries, scores = refs[2 + 3 * parts :]
    masked_pair(
        query_image[...].astype(F32), query_text[...].astype(F32), queries, HEAD ** (-0.5)
    )
    stacked = queries[...]
    top = None
    base = 0
    for part in range(parts):
        rows = key_refs[part].shape[0]
        score = dot_nt(key_refs[part][...], stacked) + bias_refs[part][...]
        scores[base : base + rows] = score
        part_top = jnp.max(score, axis=0, keepdims=True)
        top = part_top if top is None else jnp.maximum(top, part_top)
        base += rows
    total = jnp.zeros_like(top)
    attended = jnp.zeros((LANES, stacked.shape[0]), F32)
    base = 0
    for part in range(parts):
        rows = key_refs[part].shape[0]
        exponent = jnp.exp(scores[base : base + rows] - top)
        total = total + jnp.sum(exponent, axis=0, keepdims=True)
        attended = attended + dot_tn(value_refs[part][...], exponent.astype(BF16))
        base += rows
    result = unstack(attended / total)
    out_image[...] = result[:image_rows].astype(BF16)
    out_text[...] = result[image_rows:].astype(BF16)
    log_ref[...] = top + jnp.log(total)


def attend_back_kernel(streams, image_rows, *refs):
    parts = len(streams)
    query_image, query_text, out_image, out_text, grad_image, grad_text, log_ref = refs[:7]
    key_refs = refs[7 : 7 + parts]
    value_refs = refs[7 + parts : 7 + 2 * parts]
    bias_refs = refs[7 + 2 * parts : 7 + 3 * parts]
    rest = refs[7 + 3 * parts :]
    query_grad_image, query_grad_text, query_sum, value_sum = rest[:4]
    pair_grads = rest[4 : 4 + parts]
    queries, grads, products = rest[4 + parts :]
    masked_pair(
        query_image[...].astype(F32), query_text[...].astype(F32), queries, HEAD ** (-0.5)
    )
    grad_rows_image, grad_rows_text = grad_image[...].astype(F32), grad_text[...].astype(F32)
    masked_pair(grad_rows_image, grad_rows_text, grads, 1.0)
    first = lax.broadcasted_iota(jnp.int32, (1, LANES), 1) < HEAD
    product_image = grad_rows_image * out_image[...].astype(F32)
    product_text = grad_rows_text * out_text[...].astype(F32)
    half = product_image.shape[0] + product_text.shape[0]
    for head in range(2):
        kept = first if head == 0 else jnp.logical_not(first)
        base = head * half
        products[base : base + image_rows] = jnp.where(kept, product_image, 0.0)
        products[base + image_rows : base + half] = jnp.where(kept, product_text, 0.0)
    inner = jnp.sum(products[...].T, axis=0, keepdims=True)
    stacked, grad_stacked = queries[...], grads[...]
    log_total = log_ref[...]
    query_grad = jnp.zeros((LANES, stacked.shape[0]), F32)
    value_totals = [jnp.zeros((1, LANES), F32) for _ in range(2)]
    for part in range(parts):
        keys, values = key_refs[part][...], value_refs[part][...]
        probs = jnp.exp(dot_nt(keys, stacked) + bias_refs[part][...] - log_total)
        grad_probs = dot_nt(values, grad_stacked)
        grad_scores = (probs * (grad_probs - inner)).astype(BF16)
        value_grad = dot(probs.astype(BF16), grad_stacked)
        pair_grads[part][1] = value_grad.astype(BF16)
        stream = streams[part]
        value_totals[stream] = value_totals[stream] + jnp.sum(value_grad, axis=0, keepdims=True)
        pair_grads[part][0] = dot(grad_scores, stacked).astype(BF16)
        query_grad = query_grad + dot_tn(keys, grad_scores)
    result = unstack(query_grad) * HEAD ** (-0.5)
    query_grad_image[...] = result[:image_rows].astype(BF16)
    query_grad_text[...] = result[image_rows:].astype(BF16)
    query_sum[0:1] = jnp.sum(result[:image_rows], axis=0, keepdims=True)
    query_sum[1:2] = jnp.sum(result[image_rows:], axis=0, keepdims=True)
    for stream in range(2):
        value_sum[stream : stream + 1] = value_totals[stream]


def weight_kernel(groups, *refs):
    result = refs[-1]

    def body(step, carry):
        columns = pl.ds(pl.multiple_of(step * 256, 256), 256)
        base = 0
        place = 0
        for count, width in groups:
            total = None
            for _ in range(count):
                term = dot_tn(refs[place][:, columns], refs[place + 1][...])
                total = term if total is None else total + term
                place += 2
            result[columns, base : base + width] = total.astype(BF16)
            base += width
        return carry

    lax.fori_loop(0, result.shape[0] // 256, body, 0)


def weight_terms(groups):
    flat_operands = [part for group in groups for pair in group for part in pair]
    shape = tuple((len(group), group[0][1].shape[1]) for group in groups)
    rows = flat_operands[0].shape[1]
    return pl.pallas_call(
        functools.partial(weight_kernel, shape),
        in_specs=[pl.BlockSpec(memory_space=pltpu.VMEM)] * len(flat_operands),
        out_specs=pl.BlockSpec(memory_space=pltpu.VMEM),
        out_shape=jax.ShapeDtypeStruct((rows, sum(part[1] for part in shape)), BF16),
        compiler_params=pltpu.CompilerParams(vmem_limit_bytes=52 * 1024 * 1024),
        cost_estimate=LIGHT,
        name="weight_terms",
    )(*flat_operands)


def unit_parts(values):
    row_mean = jnp.mean(values, axis=-1, keepdims=True)
    centred = values - row_mean
    inverse = lax.rsqrt(jnp.mean(centred * centred, axis=-1, keepdims=True) + 1e-06)
    return centred * inverse, inverse


def middle_kernel(mine, other, tokens, mods, bias, att_ref, middle_ref, hidden_ref):
    att = mine[...].astype(F32) + other[...].astype(F32) + bias[...]
    middle = tokens[...].astype(F32) + mods[2:3] * att
    att_ref[...] = att
    middle_ref[...] = middle
    unit, _ = unit_parts(middle)
    hidden_ref[...] = (unit * (1.0 + mods[4:5]) + mods[3:4]).astype(BF16)


def add_rows(sums, values):
    @pl.when(pl.program_id(1) == 0)
    def _():
        sums[...] = jnp.zeros_like(sums)

    for place, value in enumerate(values):
        sums[place : place + 1] += jnp.sum(value, axis=0, keepdims=True)


def norm_back(values, scale, grad):
    unit, inverse = unit_parts(values)
    unit_grad = grad * (1.0 + scale)
    first = jnp.mean(unit_grad, axis=-1, keepdims=True)
    second = jnp.mean(unit_grad * unit, axis=-1, keepdims=True)
    return inverse * (unit_grad - first - unit * second), grad * unit


def middle_back_kernel(
    mine, other, middle, att, final_grad, mods, middle_grad, att_grad, sums
):
    grad = mine[...].astype(F32) + other[...].astype(F32)
    back, scaled = norm_back(middle[...], mods[4:5], grad)
    total = final_grad[...] + back
    middle_grad[...] = total
    low = total * mods[2:3]
    att_grad[...] = low.astype(BF16)
    add_rows(sums, (grad, scaled, total * att[...], low))


def edge_back_kernel(mine, other, tokens, middle_grad, mods, input_grad, sums):
    grad = mine[...].astype(F32) + other[...].astype(F32)
    back, scaled = norm_back(tokens[...].astype(F32), mods[1:2], grad)
    input_grad[...] = (middle_grad[...] + back).astype(BF16)
    add_rows(sums, (grad, scaled))


def by_rows(kernel, name, rows_arrays, slot_arrays, shared, outputs, with_sums):
    slots, rows = rows_arrays[0].shape[:2]
    step = next(size for size in (96, 72, 48, 32, 16) if rows % size == 0)
    row_spec = pl.BlockSpec((None, step, D), lambda slot, block: (slot, block, 0))
    sums_spec = pl.BlockSpec((None, 8, D), lambda slot, block: (slot, 0, 0))
    out_specs = [row_spec] * len(outputs)
    out_shape = [jax.ShapeDtypeStruct((slots, rows, D), dtype) for dtype in outputs]
    if with_sums:
        out_specs.append(sums_spec)
        out_shape.append(jax.ShapeDtypeStruct((slots, 8, D), F32))
    return pl.pallas_call(
        kernel,
        grid=(slots, rows // step),
        in_specs=[row_spec] * len(rows_arrays)
        + [
            pl.BlockSpec((None, part.shape[1], D), lambda slot, block: (slot, 0, 0))
            for part in slot_arrays
        ]
        + [pl.BlockSpec((1, D), lambda slot, block: (0, 0)) for _ in shared],
        out_specs=out_specs,
        out_shape=out_shape,
        compiler_params=pltpu.CompilerParams(vmem_limit_bytes=40 * 1024 * 1024),
        cost_estimate=LIGHT,
        name=name,
    )(*rows_arrays, *slot_arrays, *shared)


def block_of(slot, rows, base=0):
    return pl.BlockSpec((None, rows, LANES), lambda pair: (slot, 0, base + pair))


def flat_block(rows, base=0):
    return pl.BlockSpec((rows, LANES), lambda pair: (0, base + pair))


def column_block(rows):
    return pl.BlockSpec((rows, 1), lambda pair: (0, 0))


def key_specs(slot, key_parts, pairs):
    keys, values, biases = [], [], []
    for rows_array, _, here, _ in key_parts:
        rows = rows_array.shape[-2]
        if here:
            keys.append(block_of(slot, rows, pairs))
            values.append(block_of(slot, rows, 2 * pairs))
        else:
            keys.append(flat_block(rows))
            values.append(flat_block(rows, pairs))
        biases.append(column_block(rows))
    return keys + values + biases


def key_operands(key_parts):
    arrays = [part[0] for part in key_parts]
    return arrays + arrays + [part[1] for part in key_parts]


def attend(slot, width, queries, key_parts):
    image, text = queries
    image_rows, text_rows = image.shape[1], text.shape[1]
    pairs = width // LANES
    stacked = 2 * (image_rows + text_rows)
    key_rows = sum(part[0].shape[-2] for part in key_parts)
    return pl.pallas_call(
        functools.partial(attend_kernel, len(key_parts), image_rows),
        grid=(pairs,),
        in_specs=[block_of(slot, image_rows), block_of(slot, text_rows)]
        + key_specs(slot, key_parts, pairs),
        out_specs=[
            flat_block(image_rows),
            flat_block(text_rows),
            pl.BlockSpec((None, 1, stacked), lambda pair: (pair, 0, 0)),
        ],
        out_shape=[
            jax.ShapeDtypeStruct((image_rows, width), BF16),
            jax.ShapeDtypeStruct((text_rows, width), BF16),
            jax.ShapeDtypeStruct((pairs, 1, stacked), F32),
        ],
        scratch_shapes=[
            pltpu.VMEM((stacked, LANES), BF16),
            pltpu.VMEM((key_rows, stacked), F32),
        ],
        compiler_params=pltpu.CompilerParams(vmem_limit_bytes=48 * 1024 * 1024),
        cost_estimate=LIGHT,
        name="attend",
    )(image, text, *key_operands(key_parts))


def attend_back(slot, width, queries, outs, grads, log_total, key_parts):
    image, text = queries
    image_rows, text_rows = image.shape[1], text.shape[1]
    pairs = width // LANES
    stacked = 2 * (image_rows + text_rows)
    key_rows = sum(part[0].shape[-2] for part in key_parts)
    part_rows = [part[0].shape[-2] for part in key_parts]
    row_blocks = [block_of(slot, image_rows), block_of(slot, text_rows)]
    sum_block = pl.BlockSpec((None, 2, LANES), lambda pair: (pair, 0, 0))
    sum_shape = jax.ShapeDtypeStruct((pairs, 2, LANES), F32)
    return pl.pallas_call(
        functools.partial(
            attend_back_kernel, tuple(part[3] for part in key_parts), image_rows
        ),
        grid=(pairs,),
        in_specs=row_blocks
        + [flat_block(image_rows), flat_block(text_rows)]
        + [flat_block(image_rows), block_of(slot, text_rows)]
        + [pl.BlockSpec((None, 1, stacked), lambda pair: (pair, 0, 0))]
        + key_specs(slot, key_parts, pairs),
        out_specs=[flat_block(image_rows), flat_block(text_rows), sum_block, sum_block]
        + [pl.BlockSpec((2, rows, LANES), lambda pair: (0, 0, pair)) for rows in part_rows],
        out_shape=[
            jax.ShapeDtypeStruct((image_rows, width), BF16),
            jax.ShapeDtypeStruct((text_rows, width), BF16),
            sum_shape,
            sum_shape,
        ]
        + [jax.ShapeDtypeStruct((2, rows, width), BF16) for rows in part_rows],
        scratch_shapes=[
            pltpu.VMEM((stacked, LANES), BF16),
            pltpu.VMEM((stacked, LANES), BF16),
            pltpu.VMEM((stacked, LANES), F32),
        ],
        compiler_params=pltpu.CompilerParams(vmem_limit_bytes=48 * 1024 * 1024),
        cost_estimate=LIGHT,
        name="attend_back",
    )(image, text, outs[0], outs[1], grads[0], grads[1], log_total, *key_operands(key_parts))


def on_device(
    image_tokens,
    text_tokens,
    cond_vector,
    image_cotangent,
    text_cotangent,
    image_counts,
    text_counts,
    seq_live,
    ada_weight,
    ada_bias,
    qkv_weight,
    qv_bias,
    attn_out_weight,
    attn_out_bias,
    mlp_up_weight,
    mlp_up_bias,
    mlp_down_weight,
    mlp_down_bias,
):
    slot_count = image_tokens.shape[0]
    per_batch = slot_count // MB
    seq_count = seq_live.shape[0]
    cap_image = image_tokens.shape[1]
    cap_text = text_tokens.shape[1]
    text_rows = -(-cap_text // 16) * 16
    extra = ((0, 0), (0, text_rows - cap_text), (0, 0))
    caps = (cap_image, text_rows)
    group_index = lax.axis_index("z") * 2 + lax.axis_index("core")
    ctx_count = lax.axis_size("ctx")
    ctx_index = lax.axis_index("ctx")
    tp_index = lax.axis_index("tp")
    spans = 6 // lax.axis_size("tp")
    rows_local = ada_weight.shape[1]
    width = qkv_weight.shape[3]

    qkv_full = gather_rows(qkv_weight)
    out_full = gather_over_fsdp(jnp.swapaxes(attn_out_weight, 1, 2))
    up_full = gather_rows(mlp_up_weight)
    down_full = gather_rows(jnp.swapaxes(mlp_down_weight, 1, 2))

    live_all = seq_live.astype(F32)
    batch_index = jnp.arange(seq_count, dtype=jnp.int32) % slot_count // per_batch
    marked = (batch_index[:, None] == jnp.arange(MB, dtype=jnp.int32)[None, :]).astype(
        F32
    ) * live_all[:, None]
    members = jnp.sum(marked, axis=0)
    shares = jnp.sum(live_all) / (MB * jnp.maximum(members, 1.0))
    seq_weights = jnp.sum(marked * shares[None, :], axis=1)
    own_weights = lax.dynamic_slice_in_dim(seq_weights, group_index * slot_count, slot_count)
    own_live = lax.dynamic_slice_in_dim(live_all, group_index * slot_count, slot_count)

    cond_float = cond_vector.astype(F32)
    activated = jax.nn.silu(cond_float).astype(BF16)
    ada_partial = jnp.einsum("sd,tdk->stk", activated, ada_weight, preferred_element_type=F32)
    mod_half = scatter_groups(
        ada_partial.reshape(seq_count // slot_count, slot_count, 2, spans * D)
    ) + ada_bias
    mod_other = swap(mod_half, "tp")
    modulation = jnp.where(
        tp_index == 0,
        jnp.concatenate([mod_half, mod_other], axis=2),
        jnp.concatenate([mod_other, mod_half], axis=2),
    ).reshape(slot_count, 2, 6, D)

    counts = (image_counts, text_counts)
    live_rows = []
    key_bias = []
    for stream in range(2):
        places = jnp.arange(caps[stream], dtype=jnp.int32)
        own_counts = lax.dynamic_slice_in_dim(counts[stream], ctx_index, 1, 1)
        live_rows.append((places[None, :] < own_counts).astype(F32)[:, :, None])
        key_bias.append(
            jnp.where(
                places[None, None, :, None] < counts[stream][:, :, None, None], 0.0, DEAD
            ).astype(F32)
        )
    tokens = (image_tokens, jnp.pad(text_tokens, extra))
    cotangents = (image_cotangent, jnp.pad(text_cotangent, extra))

    def mod_of(stream, which):
        return modulation[:, stream, which][:, None, :]

    def flat(values):
        return values.reshape(-1, values.shape[-1])

    def tall(stream, values):
        return values.reshape(slot_count, caps[stream], values.shape[-1])

    inputs = [part.astype(F32) for part in tokens]
    hidden_in, projected = [], []
    for stream in range(2):
        normed = flat(
            modulate(inputs[stream], mod_of(stream, 0), mod_of(stream, 1)).astype(BF16)
        )
        hidden_in.append(normed)
        both_bias = qv_bias[stream].astype(F32)
        bias = jnp.concatenate([both_bias[0], jnp.zeros((width,), F32), both_bias[1]], axis=0)
        projected.append(tall(stream, (dot(normed, qkv_full[stream]) + bias).astype(BF16)))

    key_parts = []
    for slot in range(slot_count):
        parts = []
        for stream in range(2):
            if ctx_count == 2:
                other = swap(projected[stream][slot, :, width:], "ctx")
                bias = key_bias[stream][slot]
                parts.append(
                    (
                        projected[stream],
                        lax.dynamic_index_in_dim(bias, ctx_index, 0, keepdims=False),
                        True,
                        stream,
                    )
                )
                parts.append(
                    (
                        other,
                        lax.dynamic_index_in_dim(bias, 1 - ctx_index, 0, keepdims=False),
                        False,
                        stream,
                    )
                )
            else:
                everyone = lax.all_gather(
                    projected[stream][slot, :, width:], "ctx", axis=0, tiled=False
                )
                parts.append((flat(everyone), flat(key_bias[stream][slot]), False, stream))
        key_parts.append(parts)
    slots = range(slot_count)
    text_unit = slot_count

    def unit_stream(unit):
        return 1 if unit == text_unit else 0

    def unit_of(unit, values):
        if unit == text_unit:
            return values[1]
        return values[0][unit : unit + 1]

    def unit_mod(unit, which):
        return unit_of(unit, [mod_of(0, which), mod_of(1, which)])

    def unit_rows(unit, values):
        return values.reshape(-1, caps[unit_stream(unit)], values.shape[-1])

    mods = [modulation[:, 0], modulation[:, 1]]
    units = range(slot_count + 1)
    outs, logs, attended = [], [], []
    att_values, middles, hidden_units = {}, {}, {}

    def middle_of(unit, *ready):
        stream = unit_stream(unit)
        mine = dot_nt(attended[unit], out_full[stream]).astype(BF16)
        other = swap(mine, "tp")
        att_values[unit], middles[unit], hidden = by_rows(
            middle_kernel,
            "middle",
            [unit_rows(unit, after(mine, *ready)), unit_rows(unit, other), unit_of(unit, tokens)],
            [unit_of(unit, mods)],
            [attn_out_bias[stream].astype(F32)[None]],
            [F32, F32, BF16],
            False,
        )
        hidden_units[unit] = flat(hidden)

    ready = ()
    for slot in slots:
        out_image, out_text, log_total = attend(
            slot,
            width,
            [after(part, *ready) for part in projected],
            key_parts[slot],
        )
        outs.append((out_image, out_text))
        logs.append(log_total)
        attended.append(out_image)
        if slot == slot_count - 1:
            attended.append(jnp.concatenate([out[1] for out in outs], axis=0))
            middle_of(text_unit)
        middle_of(slot)
        ready = (hidden_units[slot],)
    hidden_mid = [
        jnp.concatenate([hidden_units[slot] for slot in slots], axis=0),
        hidden_units[text_unit],
    ]
    pre_acts = [dot(hidden_mid[stream], up_full[stream]) + mlp_up_bias[stream] for stream in range(2)]
    activs = [gelu_tanh(pre_act).astype(BF16) for pre_act in pre_acts]

    grad_finals, grad_mlp_low, down_bias_grads = [], [], []
    for stream in range(2):
        grad_final = (
            cotangents[stream].astype(F32) * live_rows[stream] * own_weights[:, None, None]
        )
        grad_mlp = grad_final * mod_of(stream, 5)
        grad_finals.append(grad_final)
        down_bias_grads.append(jnp.sum(flat(grad_mlp), axis=0))
        grad_mlp_low.append(flat(grad_mlp.astype(BF16)))
    def mlp_weight_term(stream, *ready):
        return dot_tn(after(grad_mlp_low[stream], *ready), activs[stream]).astype(BF16)

    def up_weight_term(stream, *ready):
        return dot_tn(after(hidden_mid[stream], *ready), pre_lows[stream]).astype(BF16)

    down_terms = [mlp_weight_term(0, activs[1])]
    down_terms.append(mlp_weight_term(1, down_terms[0]))
    pre_lows, up_bias_grads, hid2_parts = [None, None], [None, None], {}
    up_terms = [None, None]
    ready = tuple(down_terms)
    for stream in (1, 0):
        grad_act = dot(after(grad_mlp_low[stream], *ready), down_full[stream])
        pre_grad = jax.vjp(gelu_tanh, pre_acts[stream])[1](grad_act)[0]
        up_bias_grads[stream] = jnp.sum(pre_grad, axis=0)
        pre_lows[stream] = pre_grad.astype(BF16)
        for unit in units:
            if unit_stream(unit) != stream:
                continue
            rows = pre_lows[stream]
            if stream == 0:
                rows = rows[unit * cap_image : (unit + 1) * cap_image]
            hid2_parts[unit] = dot_nt(after(rows, *ready), up_full[stream]).astype(BF16)
            ready = (hid2_parts[unit],)
        if stream == 0:
            up_chip = core_step([up_terms[1]], *ready)
            ready = (up_chip,)
        else:
            up_terms[stream] = up_weight_term(stream, *ready)
            ready = (up_terms[stream],)
    down_shards = [scatter_rows(term) for term in down_terms]

    grad_middles, mid_sums, grad_att_low, grad_attended = {}, {}, {}, {}

    def middle_back(unit, *ready):
        stream = unit_stream(unit)
        other = swap(hid2_parts[unit], "tp")
        grad_middles[unit], low, mid_sums[unit] = by_rows(
            middle_back_kernel,
            "middle_back",
            [
                unit_rows(unit, after(hid2_parts[unit], *ready)),
                unit_rows(unit, other),
                middles[unit],
                att_values[unit],
                unit_of(unit, grad_finals),
            ],
            [unit_of(unit, mods)],
            [],
            [F32, BF16],
            True,
        )
        grad_att_low[unit] = flat(low)
        grad_attended[unit] = dot(grad_att_low[unit], out_full[stream]).astype(BF16)

    query_grads, given_pairs = {}, {}
    bias_sums = 0.0
    mlp_parts = []
    for slot in slots:
        middle_back(slot, *ready, *down_shards[slot : slot + 1])
        if slot == 0:
            middle_back(text_unit, grad_attended[slot])
            ready = (grad_attended[text_unit],)
        results = attend_back(
            slot,
            width,
            projected,
            outs[slot],
            (
                after(grad_attended[slot], *ready),
                tall(1, grad_attended[text_unit]),
            ),
            logs[slot],
            key_parts[slot],
        )
        ready = (results[0],)
        bias_sums = bias_sums + jnp.stack(
            [jnp.swapaxes(part, 0, 1).reshape(2, width) for part in results[2:4]], axis=1
        )
        for stream in range(2):
            query_grads[slot, stream] = results[stream]
            if ctx_count == 2:
                given_pairs[slot, stream] = (
                    results[4 + 2 * stream],
                    swap(results[5 + 2 * stream], "ctx"),
                )
            else:
                total = lax.psum_scatter(
                    results[4 + stream], "ctx", scatter_dimension=1, tiled=True
                )
                given_pairs[slot, stream] = (total, jnp.zeros_like(total))
        if slot == 0:
            up_terms[0] = up_weight_term(0, *ready)
            up_shard = scatter_rows(up_terms[0])
            ready = (up_terms[0],)
            for stream in range(2):
                rows = after(activs[stream], *ready)
                mlp_parts.append(dot_nt(rows, down_full[stream]).astype(BF16))
                ready = (mlp_parts[stream],)
            up_both = ctx_step(up_chip, *ready)

    pair_grads, hid_parts = {}, {}

    def hid_part(slot, *ready):
        for stream in range(2):
            mine, given = given_pairs[slot, stream]
            total = add_low(after(mine, *ready), given)
            pair_grads[slot, stream] = jnp.concatenate([total[0], total[1]], axis=1)
        rows = jnp.concatenate([query_grads[slot, 0], pair_grads[slot, 0]], axis=1)
        hid_parts[slot] = dot_nt(rows, qkv_full[0]).astype(BF16)

    hid_part(0, *ready)
    ready = (hid_parts[0],)
    finals, gate2_grads = [], []
    for stream in range(2):
        mlp_value = (
            tall(stream, pair_sum(mlp_parts[stream], "tp", *ready)) + mlp_down_bias[stream]
        )
        gate2_grads.append(jnp.sum(grad_finals[stream] * mlp_value, axis=1))
        middle = middles[text_unit]
        if stream == 0:
            middle = jnp.concatenate([middles[slot] for slot in slots], axis=0)
        final = (
            (middle + mod_of(stream, 5) * mlp_value)
            * live_rows[stream]
            * own_live[:, None, None]
        )
        finals.append(final.astype(BF16))
    ready = tuple(finals)
    for slot in slots[1:]:
        hid_part(slot, *ready)
        ready = (hid_parts[slot],)
    groups = []
    for stream in range(2):
        members = list(slots) if stream == 0 else [text_unit]
        groups.append(
            [(after(grad_att_low[unit], *ready, up_shard), attended[unit]) for unit in members]
        )
    for stream in range(2):
        normed = tall(stream, hidden_in[stream])
        groups.append([(normed[slot], query_grads[slot, stream]) for slot in slots])
    first_term = weight_terms(groups)
    first_shard = scatter_rows(first_term)
    ready = (first_term,)
    text_rows_grad = jnp.concatenate(
        [
            jnp.concatenate([query_grads[slot, 1], pair_grads[slot, 1]], axis=1)
            for slot in slots
        ],
        axis=0,
    )
    hid_parts[text_unit] = dot_nt(after(text_rows_grad, *ready), qkv_full[1]).astype(BF16)
    ready = (hid_parts[text_unit],)
    groups = []
    for stream in range(2):
        normed = tall(stream, hidden_in[stream])
        groups.append(
            [(after(normed[slot], *ready), pair_grads[slot, stream]) for slot in slots]
        )
    second_term = weight_terms(groups)
    second_shard = scatter_rows(second_term)
    up_mine = z_step(up_both)
    down_given = [ctx_given(after(shard, first_term)) for shard in down_shards]
    up_given = ctx_given(after(up_shard, first_term))
    ready = (second_term, up_mine, up_given, down_given[0])
    input_grads, edge_sums = {}, {}
    for unit in list(slots) + [text_unit]:
        other = swap(hid_parts[unit], "tp")
        input_grads[unit], edge_sums[unit] = by_rows(
            edge_back_kernel,
            "edge_back",
            [
                unit_rows(unit, after(hid_parts[unit], *ready)),
                unit_rows(unit, other),
                unit_of(unit, tokens),
                grad_middles[unit],
            ],
            [unit_of(unit, mods)],
            [],
            [BF16],
            True,
        )
        ready = (input_grads[unit], down_given[1])
    first_given = ctx_given(first_shard)
    down_grads = [ctx_total(*pair) for pair in zip(down_shards, down_given)]
    up_grads = [ctx_total(up_shard, up_given), end_step(up_mine)]
    first_grads = ctx_total(first_shard, first_given)
    def by_slot(values):
        image = jnp.concatenate([values[slot] for slot in slots], axis=0)
        return jnp.stack([image, values[text_unit]], axis=1)

    mod_grads = jnp.stack(
        [
            by_slot({unit: edge_sums[unit][:, 0] for unit in units}),
            by_slot({unit: edge_sums[unit][:, 1] for unit in units}),
            by_slot({unit: mid_sums[unit][:, 2] for unit in units}),
            by_slot({unit: mid_sums[unit][:, 0] for unit in units}),
            by_slot({unit: mid_sums[unit][:, 1] for unit in units}),
            jnp.stack(gate2_grads, axis=1),
        ],
        axis=2,
    )
    out_bias_sums = [
        sum(mid_sums[slot][0, 3] for slot in slots),
        jnp.sum(mid_sums[text_unit][:, 3], axis=0),
    ]
    input_grads = [
        jnp.concatenate([input_grads[slot] for slot in slots], axis=0),
        input_grads[text_unit],
    ]

    mod_half_grads = lax.dynamic_slice_in_dim(mod_grads, tp_index * spans, spans, 2)
    pieces = (
        mod_half_grads,
        bias_sums,
        jnp.stack(up_bias_grads, axis=0),
        jnp.stack(out_bias_sums, axis=0),
        jnp.stack(down_bias_grads, axis=0),
    )
    row = jnp.concatenate([piece.reshape(-1) for piece in pieces], axis=0).astype(BF16)
    row = ctx_sum(row)
    gathered = gather_groups(after(row.astype(BF16), first_shard))
    second_shard = after(second_shard, gathered)
    second_grads = ctx_total(second_shard, ctx_given(second_shard))
    out_grads = [first_grads[:, :width], first_grads[:, width : 2 * width]]
    q_weight_grads = [first_grads[:, 2 * width : 3 * width], first_grads[:, 3 * width :]]
    kv_weight_grads = [second_grads[:, : 2 * width], second_grads[:, 2 * width :]]
    everyone = gathered.astype(F32)
    ends = []
    base = 0
    for piece in pieces:
        ends.append(everyone[:, base : base + piece.size].reshape((-1,) + piece.shape))
        base += piece.size
    mod_all = ends[0].reshape(seq_count, 2, spans * D)
    qv_bias_grad, up_bias_grad, out_bias_grad, down_bias_grad = [
        jnp.sum(part, axis=0) for part in ends[1:]
    ]
    ada_bias_grad = jnp.sum(mod_all, axis=0)
    mod_low = mod_all.astype(BF16)
    ada_weight_grad = jnp.einsum(
        "sd,stk->tdk", activated, mod_low, preferred_element_type=F32
    )
    silu_part = jnp.einsum("stk,tdk->sd", mod_low, ada_weight, preferred_element_type=F32)
    cond_grad = jax.vjp(jax.nn.silu, cond_float)[1](pair_sum(silu_part, "tp"))[0]
    qkv_grad = jnp.stack(
        [
            jnp.concatenate(
                [q_weight_grads[stream][:, None], kv_weight_grads[stream].reshape(-1, 2, width)],
                axis=1,
            )
            for stream in range(2)
        ],
        axis=0,
    )
    return (
        finals[0],
        finals[1][:, :cap_text],
        input_grads[0],
        input_grads[1][:, :cap_text],
        cond_grad,
        ada_weight_grad,
        ada_bias_grad,
        qkv_grad,
        qv_bias_grad,
        jnp.stack([part.T for part in out_grads], axis=0),
        out_bias_grad,
        jnp.stack(up_grads, axis=0),
        up_bias_grad,
        jnp.stack([part.T for part in down_grads], axis=0),
        down_bias_grad,
    )


def solution(mesh):
    fsdp, ctx, tp = (mesh.shape[name] for name in ("fsdp", "ctx", "tp"))
    split = Mesh(mesh.devices.reshape(fsdp // 2, 2, ctx, tp), ("z", "core", "ctx", "tp"))
    rows = P(FSDP, "ctx", None)
    inner = P(None, FSDP, "tp")
    outer = P(None, "tp", FSDP)
    return jax.shard_map(
        on_device,
        mesh=split,
        in_specs=(
            rows,
            rows,
            P(None, FSDP),
            rows,
            rows,
            P(FSDP, None),
            P(FSDP, None),
            P(),
            inner,
            P(None, "tp"),
            P(None, FSDP, None, "tp"),
            P(None, None, "tp"),
            outer,
            P(),
            inner,
            P(None, "tp"),
            outer,
            P(),
        ),
        out_specs=(
            rows,
            rows,
            rows,
            rows,
            P(None, FSDP),
            inner,
            P(None, "tp"),
            P(None, FSDP, None, "tp"),
            P(None, None, "tp"),
            outer,
            P(),
            inner,
            P(None, "tp"),
            outer,
            P(),
        ),
        check_vma=False,
    )
```
